32 devices in a mesh: ctx: 4 (over y, x), tp: 8 (over z, core).
Axes of the slice: x: 2, y: 2, z: 4, core: 2. Of those that a mesh axis runs over, the one named last changes fastest.
Arguments:
- resid_in: bfloat16 [512, 1024], P('ctx', 'tp'), may hold values from -6 to 6
- feats: bfloat16 [512, 3, 1024], P('ctx', None, 'tp'), may hold values from -6 to 6
- short_filter: float32 [3, 3, 1024], P(None, None, 'tp'), may hold values from -3.5 to 3.5
- residues: float32 [1024, 16], P('tp'), may hold values from -4 to 4
- rates: float32 [1024, 16], P('tp'), may hold values from 0.0005859375 to 0.03
- out_weight: bfloat16 [1024, 1024], P('tp'), may hold values from -0.25 to 0.25
- norm_gain: float32 [1024], replicated, may hold values from 0.1 to 1.9
- attn_weight: bfloat16 [1024, 3, 1024], P(None, None, 'tp'), may hold values from -1 to 1
Outputs:
- hyena_out: bfloat16 [512, 1024], P('ctx', 'tp')
- context: bfloat16 [512, 1024], P('ctx', 'tp')
The draws below stay inside these ranges and needn't reach their ends.
All inputs are finite; a program needn't handle non-finite values.
Results may differ from the reference program's by a relative error of at most 0.01.
Values may be sent and summed in bfloat16 or wider, within the bound.
A program may use at most 192 MiB of HBM per device.

```python
import math
import jax
import jax.numpy as jnp
from jax import lax

HEAD_DIM = 128
MODES = 16
D = 1024
SEQ = 512


def draw_attn_weight(key, part):
    first_key = jax.random.fold_in(jax.random.fold_in(key, 7), 0)
    joined = jax.random.normal(first_key, (D, 3, D), jnp.float32) / math.sqrt(D)
    return jnp.clip(joined, -1.0, 1.0).astype(jnp.bfloat16)


def raised(values, rng, source, target, blocks, factor):
    def block_of(dim):
        return (jnp.arange(values.shape[dim]) // (values.shape[dim] // blocks)).reshape((-1,) + (1,) * (values.ndim - 1 - dim))

    one_side = jax.random.permutation(rng, blocks)[block_of(target)]
    other_side = (block_of(target) + blocks // 2) % blocks
    return jnp.where((block_of(source) == one_side) | (block_of(source) == other_side), factor * values, values)


def block_levels(stream_key, dims, cuts, smallest, high):
    level = 1.0
    for position, blocks in cuts:
        heights = jax.random.uniform(jax.random.fold_in(jax.random.fold_in(stream_key, 6), position), (blocks,), jnp.float32, smallest / len(cuts), high / len(cuts))
        level = level * jnp.repeat(jnp.exp(heights), dims[position] // blocks).reshape((-1,) + (1,) * (len(dims) - 1 - position))
    return level


def scatter_about(rng, dims, scale, reach, shards=(), held_as=jnp.bfloat16):
    array = jax.random.normal(rng, dims, jnp.float32) * scale
    if len(shards) > 0:
        array = block_levels(rng, dims, shards, -0.22, 0.18) * array
    return jnp.clip(array, min=-reach, max=reach).astype(held_as)


def noise_with(own_key, dims, scale, bound, shards, heavy, held_as=jnp.bfloat16):
    result = scale * jax.random.normal(own_key, dims, jnp.float32)
    if shards:
        result = result * block_levels(own_key, dims, shards, -0.22, 0.18)
    return jnp.clip(raised(result, jax.random.fold_in(own_key, 3), *heavy), -bound, bound).astype(held_as)


def setup_inputs(seed: int = 0) -> dict:
    splits = jax.random.split(jax.random.key(seed), 9)
    resid_in = scatter_about(splits[0], (SEQ, D), 1.0, 6.0, ((0, 4), (1, 8)))
    feats = scatter_about(splits[1], (SEQ, 3, D), 1.0, 6.0, ((0, 4), (2, 8)))
    short_filter = scatter_about(splits[2], (3, 3, D), 3 ** -0.5, 3.5, ((2, 8),), jnp.float32)
    residues = scatter_about(splits[3], (D, MODES), 0.25, 4.0, ((0, 8),), jnp.float32)
    rates = jnp.clip(jnp.exp(math.log(0.03) - 3.9357395 * jax.random.uniform(splits[4], (D, MODES), jnp.float32) ** block_levels(splits[4], (D, MODES), ((0, 8),), -0.2, 0.2)), 0.0005859375, 0.03)
    out_weight = noise_with(splits[5], (D, D), D ** -0.5, 0.25, ((0, 8),), (0, 1, 8, 2.0))
    norm_gain = jnp.clip(1.0 + 0.18 * jax.random.normal(splits[6], (D,), jnp.float32), 0.1, 1.9)
    attn_weight = draw_attn_weight(jax.random.fold_in(splits[8], 71), 0)
    return {"resid_in": resid_in, "feats": feats, "short_filter": short_filter, "residues": residues, "rates": rates, "out_weight": out_weight, "norm_gain": norm_gain, "attn_weight": attn_weight}


def long_conv(signal, residues, rates):
    seq_total, width_all = signal.shape
    block_size = math.gcd(width_all, 256)
    block_count = width_all // block_size
    lag_steps = jnp.arange(seq_total, dtype=jnp.float32)
    fft_size = 2 * seq_total

    def one_block(slot_item):
        sig_block, res_block, rate_block = slot_item
        weight = res_block * jnp.sqrt(1.0 - jnp.exp(-2.0 * rate_block))
        filter_taps = lax.optimization_barrier(jnp.sum(weight[:, :, None] * jnp.exp(-rate_block[:, :, None] * lag_steps), axis=1))
        spectrum = jnp.fft.rfft(sig_block.T.astype(jnp.float32), n=fft_size) * jnp.fft.rfft(filter_taps, n=fft_size)
        return jnp.fft.irfft(spectrum, n=fft_size)[:, :seq_total]
    sig_parts = signal.reshape(seq_total, block_count, block_size).transpose(1, 0, 2)
    res_parts = residues.reshape(block_count, block_size, residues.shape[1])
    rate_parts = rates.reshape(block_count, block_size, rates.shape[1])
    outputs = lax.map(one_block, (sig_parts, res_parts, rate_parts))
    return outputs.transpose(2, 0, 1).reshape(seq_total, width_all)

def rotary_turn(vectors, positions):
    half_dim = vectors.shape[-1] // 2
    frequency = 10000.0 ** (-jnp.arange(half_dim, dtype=jnp.float32) * 2.0 / vectors.shape[-1])
    angles = positions.astype(jnp.float32)[:, None] * frequency[None, :]
    cosine = jnp.cos(angles)[:, None, :]
    sine_part = jnp.sin(angles)[:, None, :]
    first_half = vectors[..., :half_dim]
    second = vectors[..., half_dim:]
    return jnp.concatenate([first_half * cosine - second * sine_part, second * cosine + first_half * sine_part], axis=-1)

def reference(resid_in, feats, short_filter, residues, rates, out_weight, norm_gain, attn_weight):
    seq_total = feats.shape[0]
    width_all = feats.shape[2]
    as_float = feats.astype(jnp.float32)
    padded = jnp.concatenate([jnp.zeros((2, 3, width_all), jnp.float32), as_float], axis=0)
    short_out = short_filter[0] * padded[2:] + short_filter[1] * padded[1:seq_total + 1] + short_filter[2] * padded[:seq_total]
    product = (short_out[:, 1] * short_out[:, 2]).astype(jnp.bfloat16)
    conv_out = long_conv(product, residues, rates)
    gated = (short_out[:, 0] * conv_out).astype(jnp.bfloat16)
    mix = jnp.dot(gated, out_weight, preferred_element_type=jnp.float32)
    hyena_out = (resid_in.astype(jnp.float32) + mix).astype(jnp.bfloat16)
    wide = hyena_out.astype(jnp.float32)
    mean_square = lax.optimization_barrier(jnp.mean(wide * wide, axis=1, keepdims=True))
    normed = (wide * lax.rsqrt(mean_square + 1e-05) * norm_gain).astype(jnp.bfloat16)
    projected = jnp.dot(normed, attn_weight.reshape(width_all, 3 * width_all), preferred_element_type=jnp.float32).reshape(seq_total, 3, width_all)
    head_count = width_all // HEAD_DIM
    positions = jnp.arange(seq_total, dtype=jnp.int32)
    queries = rotary_turn(projected[:, 0].reshape(seq_total, head_count, HEAD_DIM), positions).astype(jnp.bfloat16)
    keys_all = rotary_turn(projected[:, 1].reshape(seq_total, head_count, HEAD_DIM), positions).astype(jnp.bfloat16)
    values = projected[:, 2].reshape(seq_total, head_count, HEAD_DIM).astype(jnp.bfloat16)
    score_scale = 1.0 / math.sqrt(HEAD_DIM)
    block_size = math.gcd(seq_total, 1024)
    block_count = seq_total // block_size
    key_pos = jnp.arange(seq_total, dtype=jnp.int32)

    def one_head(slot_item):
        head_queries, head_keys, head_values = slot_item
        query_blocks = head_queries.reshape(block_count, block_size, HEAD_DIM)

        def one_block(pair_item):
            query_block, block_index = pair_item
            scores = jnp.dot(query_block, head_keys.T, preferred_element_type=jnp.float32) * score_scale
            query_pos = block_index * block_size + jnp.arange(block_size, dtype=jnp.int32)
            allowed = query_pos[:, None] >= key_pos[None, :]
            masked = jnp.where(allowed, scores, -1e+30)
            run_peak = lax.optimization_barrier(jnp.max(masked, axis=1, keepdims=True))
            probs = jnp.where(allowed, jnp.exp(masked - run_peak), 0.0)
            denom = lax.optimization_barrier(jnp.sum(probs, axis=1, keepdims=True))
            summed = jnp.dot(probs.astype(jnp.bfloat16), head_values, preferred_element_type=jnp.float32)
            return summed / denom
        outputs = lax.map(one_block, (query_blocks, jnp.arange(block_count, dtype=jnp.int32)))
        return outputs.reshape(seq_total, HEAD_DIM)
    per_head = lax.map(one_head, (queries.transpose(1, 0, 2), keys_all.transpose(1, 0, 2), values.transpose(1, 0, 2)))
    context = per_head.transpose(1, 0, 2).reshape(seq_total, width_all).astype(jnp.bfloat16)
    return (hyena_out, context)
```

```python
import functools
import math

import jax
import jax.numpy as jnp
import numpy as np
from jax import lax
from jax.experimental import pallas as pl
from jax.experimental.pallas import tpu as pltpu
from jax.sharding import PartitionSpec as P

HEAD_DIM = 128
EPS = 1e-05
ROPE_BASE = 10000.0
FILL = -1e30
MESH = pl.DeviceIdType.MESH
F32 = jnp.float32
BF16 = jnp.bfloat16


def kernel(
    n_ctx,
    n_tp,
    resid_ref,
    feats_ref,
    sf_ref,
    res_ref,
    rate_ref,
    gain_ref,
    table_ref,
    base_ref,
    ow_hbm,
    aw_hbm,
    hy_ref,
    ctx_ref,
    ow,
    aw,
    xpad,
    prod,
    fsh,
    msg,
    msg_in,
    part_out,
    part_in,
    gath,
    kv,
    scores,
    w_sem,
    s1,
    r1,
    s2,
    r2,
    s3,
    r3,
    s4,
    r4,
):
    me_c = lax.axis_index("ctx")
    me_t = lax.axis_index("tp")
    rows = resid_ref.shape[0]
    modes = res_ref.shape[0]
    width = n_tp * 128
    tiles = rows // 8

    barrier = pltpu.get_barrier_semaphore()
    for d in range(1, n_tp):
        peer = lax.rem(me_t + d, n_tp)
        pl.semaphore_signal(barrier, inc=1, device_id={"tp": peer}, device_id_type=MESH)
    for d in range(1, n_ctx):

        @pl.when(me_c >= d)
        def _(d=d):
            pl.semaphore_signal(
                barrier, inc=1, device_id={"ctx": me_c - d}, device_id_type=MESH
            )

    w_copies = [pltpu.make_async_copy(ow_hbm, ow, w_sem.at[0])]
    for slot, p in enumerate((1, 2, 0)):
        w_copies.append(
            pltpu.make_async_copy(
                aw_hbm.at[p], aw.at[:, pl.ds(slot * 128, 128)], w_sem.at[1 + slot]
            )
        )
    for c in w_copies:
        c.start()

    short = []
    for p in range(3):
        x = feats_ref[p].astype(F32)
        xpad[p, 0:8, :] = jnp.zeros((8, 128), F32)
        xpad[p, pl.ds(8, rows), :] = x
        short.append(
            sf_ref[0, p : p + 1, :] * x
            + sf_ref[1, p : p + 1, :] * xpad[p, pl.ds(7, rows), :]
            + sf_ref[2, p : p + 1, :] * xpad[p, pl.ds(6, rows), :]
        )
    row_id = lax.broadcasted_iota(jnp.int32, (rows, 128), 0)
    p_mask = jnp.where(row_id >= 2, (short[1] * short[2]).astype(BF16).astype(F32), 0.0)
    prod[...] = p_mask

    rates = rate_ref[...]
    eight = lax.broadcasted_iota(jnp.int32, (8, 128), 0).astype(F32)
    lam8 = jnp.exp(-8.0 * rates)

    for m in range(modes):
        state = p_mask[0:8]
        for i in range(1, tiles):
            state = state * lam8[m : m + 1] + p_mask[8 * i : 8 * i + 8]
        state = state * jnp.exp(-rates[m : m + 1] * (7.0 - eight))
        msg[m : m + 1, :] = jnp.sum(state, axis=0, keepdims=True)
    for p in range(3):
        msg[16 + 2 * p : 18 + 2 * p, :] = xpad[p, rows + 6 : rows + 8, :]
    for p in range(1, 3):
        msg[20 + 2 * p : 22 + 2 * p, :] = xpad[p, 8:10, :]
    msg[26:32, :] = jnp.zeros((6, 128), F32)

    pl.semaphore_wait(barrier, n_tp - 1 + (n_ctx - 1 - me_c))

    def msg_copy(d):
        return pltpu.make_async_remote_copy(
            src_ref=msg,
            dst_ref=msg_in.at[me_c],
            send_sem=s1.at[d],
            recv_sem=r1.at[me_c],
            device_id={"ctx": me_c + d},
            device_id_type=MESH,
        )

    for d in range(1, n_ctx):

        @pl.when(me_c + d < n_ctx)
        def _(d=d):
            msg_copy(d).start()

    weight = res_ref[...] * jnp.sqrt(1.0 - jnp.exp(-2.0 * rates))
    taps = [jnp.zeros((8, 128), F32) for _ in range(tiles)]
    for m in range(modes):
        e = weight[m : m + 1] * jnp.exp(-rates[m : m + 1] * eight)
        for i in range(tiles):
            taps[i] = taps[i] + e
            e = e * lam8[m : m + 1]
    taps = jnp.concatenate(taps, axis=0)
    for r in range(8):
        fsh[r, 0 : rows + 8, :] = jnp.zeros((rows + 8, 128), F32)
        fsh[r, rows + r : 2 * rows, :] = taps[0 : rows - r]

    def conv_step(j, acc):
        start = pl.multiple_of(rows - 8 * j, 8)
        block = prod[pl.ds(pl.multiple_of(8 * j, 8), 8), :]
        for r in range(8):
            acc = acc + fsh[r, pl.ds(start, rows), :] * block[r : r + 1]
        return acc

    conv = lax.fori_loop(0, tiles, conv_step, jnp.zeros((rows, 128), F32))

    cos_l, sin_l = table_ref[0], table_ref[1]
    cos_b = base_ref[0, pl.ds(me_c, 1), :]
    sin_b = base_ref[1, pl.ds(me_c, 1), :]
    lane = lax.broadcasted_iota(jnp.int32, (rows, 128), 1)
    cosine = cos_b * cos_l - sin_b * sin_l
    sine = sin_b * cos_l + cos_b * sin_l
    sine = jnp.where(lane < 64, -sine, sine)

    span = float(rows)
    lam_full = jnp.exp(-span * rates)
    lam_p0 = jnp.exp(-(span - 1.0) * rates)
    lam_p1 = jnp.exp(-(span - 2.0) * rates)

    def tap(j, p):
        return sf_ref[j, p : p + 1, :]

    def first_rows(p, x0, x1, h0, h1):
        a = tap(0, p) * x0 + tap(1, p) * h1 + tap(2, p) * h0
        b = tap(0, p) * x1 + tap(1, p) * x0 + tap(2, p) * h1
        return a, b

    def first_products(kx, vx, halo):
        k0, k1 = first_rows(1, kx[0], kx[1], halo[2], halo[3])
        v0, v1 = first_rows(2, vx[0], vx[1], halo[4], halo[5])
        return (k0 * v0).astype(BF16).astype(F32), (k1 * v1).astype(BF16).astype(F32)

    def state_step(k, carried):
        total, halo = carried
        pltpu.make_async_remote_copy(
            src_ref=msg,
            dst_ref=msg_in.at[k],
            send_sem=s1.at[0],
            recv_sem=r1.at[k],
            device_id={"ctx": k},
            device_id_type=MESH,
        ).wait_recv()
        got = [msg_in[k, i : i + 1, :] for i in range(16, 26)]
        p0, p1 = first_products(got[6:8], got[8:10], halo)
        total = total * lam_full + msg_in[k, 0:modes, :] + lam_p0 * p0 + lam_p1 * p1
        return total, tuple(got[0:6])

    zero_row = jnp.zeros((1, 128), F32)
    total, halo = lax.fori_loop(
        0, me_c, state_step, (jnp.zeros((modes, 128), F32), (zero_row,) * 6)
    )
    p0, p1 = first_products(
        [xpad[1, 8:9, :], xpad[1, 9:10, :]], [xpad[2, 8:9, :], xpad[2, 9:10, :]], halo
    )
    q0, q1 = first_rows(0, xpad[0, 8:9, :], xpad[0, 9:10, :], halo[0], halo[1])
    total = total * weight
    cross = [jnp.zeros((8, 128), F32) for _ in range(tiles)]
    for m in range(modes):
        e = total[m : m + 1] * jnp.exp(-rates[m : m + 1] * (eight + 1.0))
        for i in range(tiles):
            cross[i] = cross[i] + e
            e = e * lam8[m : m + 1]
    conv = conv + jnp.concatenate(cross, axis=0)
    conv = conv + fsh[0, pl.ds(rows, rows), :] * p0 + fsh[1, pl.ds(rows, rows), :] * p1
    query_part = jnp.where(row_id == 0, q0, jnp.where(row_id == 1, q1, short[0]))
    gated = (query_part * conv).astype(BF16)

    w_copies[0].wait()

    def part_copy(d, target):
        return pltpu.make_async_remote_copy(
            src_ref=part_out.at[d],
            dst_ref=part_in.at[d],
            send_sem=s2.at[d],
            recv_sem=r2.at[d],
            device_id={"tp": target},
            device_id_type=MESH,
        )

    def columns(t):
        return ow[:, pl.ds(pl.multiple_of(t * 128, 128), 128)]

    for d in range(1, n_tp):
        peer = lax.rem(me_t + d, n_tp)
        part_out[d] = jnp.dot(gated, columns(peer), preferred_element_type=F32).astype(BF16)
        part_copy(d, peer).start()
    mix = jnp.dot(gated, columns(me_t), preferred_element_type=F32)
    for d in range(1, n_tp):
        part_copy(d, me_t).wait_recv()
        mix = mix + part_in[d].astype(F32)
    hyena = (resid_ref[...].astype(F32) + mix).astype(BF16)
    gath[me_t] = hyena

    def gath_copy(d, owner, target):
        return pltpu.make_async_remote_copy(
            src_ref=gath.at[owner],
            dst_ref=gath.at[owner],
            send_sem=s3.at[d],
            recv_sem=r3.at[d],
            device_id={"tp": target},
            device_id_type=MESH,
        )

    for d in range(1, n_tp):
        gath_copy(d, me_t, lax.rem(me_t + d, n_tp)).start()
    hy_ref[...] = hyena
    for d in range(1, n_tp):
        gath_copy(d, lax.rem(me_t + n_tp - d, n_tp), me_t).wait_recv()
    wide = [gath[j].astype(F32) for j in range(n_tp)]
    square = wide[0] * wide[0]
    for j in range(1, n_tp):
        square = square + wide[j] * wide[j]
    scale = lax.rsqrt(jnp.sum(square, axis=1, keepdims=True) / float(width) + EPS)
    normed = jnp.concatenate(
        [(wide[j] * scale * gain_ref[j : j + 1, :]).astype(BF16) for j in range(n_tp)], axis=1
    )
    for c in w_copies[1:]:
        c.wait()

    def turned(x):
        return (x * cosine + pltpu.roll(x, 64, axis=1) * sine).astype(BF16)

    key_value = jnp.dot(normed, aw[:, 0:256], preferred_element_type=F32)
    kv[0, me_c] = turned(key_value[:, 0:128])
    kv[1, me_c] = key_value[:, 128:256].astype(BF16)

    def kv_copy(which, d, owner, target):
        return pltpu.make_async_remote_copy(
            src_ref=kv.at[which, owner],
            dst_ref=kv.at[which, owner],
            send_sem=s4.at[which, d],
            recv_sem=r4.at[which, owner],
            device_id={"ctx": target},
            device_id_type=MESH,
        )

    for which in range(2):
        for d in range(1, n_ctx):

            @pl.when(me_c + d < n_ctx)
            def _(which=which, d=d):
                kv_copy(which, d, me_c, me_c + d).start()

    queries = turned(jnp.dot(normed, aw[:, 256:384], preferred_element_type=F32))
    factor = 1.0 / math.sqrt(HEAD_DIM)

    def score_of(k):
        return (
            lax.dot_general(
                queries, kv[0, k], (((1,), (1,)), ((), ())), preferred_element_type=F32
            )
            * factor
        )

    own = jnp.where(row_id >= lane, score_of(me_c), FILL)

    def score_step(k, peak):
        kv_copy(0, 0, k, k).wait_recv()
        s = score_of(k)
        scores[k] = s
        return jnp.maximum(peak, s)

    peak = jnp.max(lax.fori_loop(0, me_c, score_step, own), axis=1, keepdims=True)
    probs = jnp.where(row_id >= lane, jnp.exp(own - peak), 0.0)
    acc = jnp.dot(probs.astype(BF16), kv[1, me_c], preferred_element_type=F32)

    def value_step(k, carried):
        total_p, total_v = carried
        kv_copy(1, 0, k, k).wait_recv()
        pr = jnp.exp(scores[k] - peak)
        total_v = total_v + jnp.dot(pr.astype(BF16), kv[1, k], preferred_element_type=F32)
        return total_p + pr, total_v

    probs, acc = lax.fori_loop(0, me_c, value_step, (probs, acc))
    ctx_ref[...] = (acc / jnp.sum(probs, axis=1, keepdims=True)).astype(BF16)

    for d in range(1, n_tp):
        part_copy(d, me_t).wait_send()
        gath_copy(d, me_t, me_t).wait_send()
    for d in range(1, n_ctx):

        @pl.when(me_c + d < n_ctx)
        def _(d=d):
            msg_copy(d).wait_send()
            kv_copy(0, d, me_c, me_c + d).wait_send()
            kv_copy(1, d, me_c, me_c + d).wait_send()


def rotary_tables(rows, n_ctx):
    half = HEAD_DIM // 2
    freq = ROPE_BASE ** (-np.arange(half, dtype=np.float64) * 2.0 / HEAD_DIM)
    freq = np.concatenate([freq, freq])
    local = np.arange(rows)[:, None] * freq
    base = (np.arange(n_ctx) * rows)[:, None] * freq
    table = np.stack([np.cos(local), np.sin(local)]).astype(np.float32)
    return table, np.stack([np.cos(base), np.sin(base)]).astype(np.float32)


def solution(mesh):
    n_ctx, n_tp = mesh.shape["ctx"], mesh.shape["tp"]

    def per_device(resid, feats, sf, residues, rates, ow, gain, aw):
        rows = resid.shape[0]
        width = ow.shape[1]
        table, base = rotary_tables(rows, n_ctx)
        vmem = pl.BlockSpec(memory_space=pltpu.VMEM)
        hbm = pl.BlockSpec(memory_space=pltpu.HBM)
        dma = pltpu.SemaphoreType.DMA
        block = (rows, 128)
        return pl.pallas_call(
            functools.partial(kernel, n_ctx, n_tp),
            out_shape=(
                jax.ShapeDtypeStruct(block, BF16),
                jax.ShapeDtypeStruct(block, BF16),
            ),
            in_specs=[vmem] * 8 + [hbm] * 2,
            out_specs=(vmem, vmem),
            scratch_shapes=[
                pltpu.VMEM(ow.shape, BF16),
                pltpu.VMEM((width, 384), BF16),
                pltpu.VMEM((3, rows + 8, 128), F32),
                pltpu.VMEM(block, F32),
                pltpu.VMEM((8, 2 * rows, 128), F32),
                pltpu.VMEM((32, 128), F32),
                pltpu.VMEM((n_ctx, 32, 128), F32),
                pltpu.VMEM((n_tp,) + block, BF16),
                pltpu.VMEM((n_tp,) + block, BF16),
                pltpu.VMEM((n_tp,) + block, BF16),
                pltpu.VMEM((2, n_ctx) + block, BF16),
                pltpu.VMEM((n_ctx,) + block, F32),
                dma((4,)),
                dma((n_ctx,)),
                dma((n_ctx,)),
                dma((n_tp,)),
                dma((n_tp,)),
                dma((n_tp,)),
                dma((n_tp,)),
                dma((2, n_ctx)),
                dma((2, n_ctx)),
            ],
            compiler_params=pltpu.CompilerParams(
                collective_id=0, has_side_effects=True, vmem_limit_bytes=40 * 1024 * 1024
            ),
        )(
            resid,
            feats.transpose(1, 0, 2),
            sf,
            residues.T,
            rates.T,
            gain.reshape(n_tp, 128),
            jnp.asarray(table),
            jnp.asarray(base),
            ow,
            aw.transpose(1, 0, 2),
        )

    in_specs = (
        P("ctx", "tp"),
        P("ctx", None, "tp"),
        P(None, None, "tp"),
        P("tp", None),
        P("tp", None),
        P("tp", None),
        P(),
        P(None, None, "tp"),
    )
    return jax.shard_map(
        per_device,
        mesh=mesh,
        in_specs=in_specs,
        out_specs=(P("ctx", "tp"), P("ctx", "tp")),
        check_vma=False,
    )
```

```python
import functools
import math

import jax
import jax.numpy as jnp
import numpy as np
from jax import lax
from jax.experimental import pallas as pl
from jax.experimental.pallas import tpu as pltpu
from jax.sharding import PartitionSpec as P

HEAD_DIM = 128
EPS = 1e-05
ROPE_BASE = 10000.0
FILL = -1e30
MESH = pl.DeviceIdType.MESH
F32 = jnp.float32
BF16 = jnp.bfloat16


def kernel(
    n_ctx,
    n_tp,
    resid_hbm,
    feats_hbm,
    sf_hbm,
    res_hbm,
    rate_hbm,
    gain_hbm,
    table_hbm,
    base_hbm,
    ow_hbm,
    aw_hbm,
    hy_ref,
    ctx_ref,
    resid_ref,
    feats_ref,
    sf_ref,
    res_ref,
    rate_ref,
    gain_ref,
    table_ref,
    base_ref,
    ow,
    aw,
    xpad,
    prod,
    fsh,
    msg,
    msg_in,
    part_out,
    part_in,
    gath,
    kv,
    scores,
    w_sem,
    in_sem,
    s1,
    r1,
    s2,
    r2,
    s3,
    r3,
    s4,
    r4,
):
    me_c = lax.axis_index("ctx")
    me_t = lax.axis_index("tp")
    rows = resid_ref.shape[0]
    modes = res_ref.shape[0]
    width = n_tp * 128
    tiles = rows // 8

    in_copies = []
    for i, (src, dst) in enumerate(
        (
            (feats_hbm, feats_ref),
            (sf_hbm, sf_ref),
            (rate_hbm, rate_ref),
            (res_hbm, res_ref),
            (table_hbm, table_ref),
            (base_hbm, base_ref),
            (resid_hbm, resid_ref),
            (gain_hbm, gain_ref),
        )
    ):
        in_copies.append(pltpu.make_async_copy(src, dst, in_sem.at[i]))
    for c in in_copies:
        c.start()

    barrier = pltpu.get_barrier_semaphore()
    for d in range(1, n_tp):
        peer = lax.rem(me_t + d, n_tp)
        pl.semaphore_signal(barrier, inc=1, device_id={"tp": peer}, device_id_type=MESH)
    for d in range(1, n_ctx):

        @pl.when(me_c >= d)
        def _(d=d):
            pl.semaphore_signal(
                barrier, inc=1, device_id={"ctx": me_c - d}, device_id_type=MESH
            )

    w_copies = [pltpu.make_async_copy(ow_hbm, ow, w_sem.at[0])]
    for slot, p in enumerate((1, 2, 0)):
        w_copies.append(
            pltpu.make_async_copy(
                aw_hbm.at[p], aw.at[:, pl.ds(slot * 128, 128)], w_sem.at[1 + slot]
            )
        )
    for c in w_copies:
        c.start()

    for c in in_copies[0:3]:
        c.wait()

    short = []
    for p in range(3):
        x = feats_ref[p].astype(F32)
        xpad[p, 0:8, :] = jnp.zeros((8, 128), F32)
        xpad[p, pl.ds(8, rows), :] = x
        short.append(
            sf_ref[0, p : p + 1, :] * x
            + sf_ref[1, p : p + 1, :] * xpad[p, pl.ds(7, rows), :]
            + sf_ref[2, p : p + 1, :] * xpad[p, pl.ds(6, rows), :]
        )
    row_id = lax.broadcasted_iota(jnp.int32, (rows, 128), 0)
    p_mask = jnp.where(row_id >= 2, (short[1] * short[2]).astype(BF16).astype(F32), 0.0)
    prod[...] = p_mask

    rates = rate_ref[...]
    eight = lax.broadcasted_iota(jnp.int32, (8, 128), 0).astype(F32)
    lam8 = jnp.exp(-8.0 * rates)

    for m in range(modes):
        state = p_mask[0:8]
        for i in range(1, tiles):
            state = state * lam8[m : m + 1] + p_mask[8 * i : 8 * i + 8]
        state = state * jnp.exp(-rates[m : m + 1] * (7.0 - eight))
        msg[m : m + 1, :] = jnp.sum(state, axis=0, keepdims=True)
    for p in range(3):
        msg[16 + 2 * p : 18 + 2 * p, :] = xpad[p, rows + 6 : rows + 8, :]
    for p in range(1, 3):
        msg[20 + 2 * p : 22 + 2 * p, :] = xpad[p, 8:10, :]
    msg[26:32, :] = jnp.zeros((6, 128), F32)

    pl.semaphore_wait(barrier, n_tp - 1 + (n_ctx - 1 - me_c))

    def msg_copy(d):
        return pltpu.make_async_remote_copy(
            src_ref=msg,
            dst_ref=msg_in.at[me_c],
            send_sem=s1.at[d],
            recv_sem=r1.at[me_c],
            device_id={"ctx": me_c + d},
            device_id_type=MESH,
        )

    for d in range(1, n_ctx):

        @pl.when(me_c + d < n_ctx)
        def _(d=d):
            msg_copy(d).start()

    for c in in_copies[3:]:
        c.wait()
    weight = res_ref[...] * jnp.sqrt(1.0 - jnp.exp(-2.0 * rates))
    taps = [jnp.zeros((8, 128), F32) for _ in range(tiles)]
    for m in range(modes):
        e = weight[m : m + 1] * jnp.exp(-rates[m : m + 1] * eight)
        for i in range(tiles):
            taps[i] = taps[i] + e
            e = e * lam8[m : m + 1]
    taps = jnp.concatenate(taps, axis=0)
    for r in range(8):
        fsh[r, 0 : rows + 8, :] = jnp.zeros((rows + 8, 128), F32)
        fsh[r, rows + r : 2 * rows, :] = taps[0 : rows - r]

    def conv_step(j, acc):
        start = pl.multiple_of(rows - 8 * j, 8)
        block = prod[pl.ds(pl.multiple_of(8 * j, 8), 8), :]
        for r in range(8):
            acc = acc + fsh[r, pl.ds(start, rows), :] * block[r : r + 1]
        return acc

    conv = lax.fori_loop(0, tiles, conv_step, jnp.zeros((rows, 128), F32))

    cos_l, sin_l = table_ref[0], table_ref[1]
    cos_b = base_ref[0, pl.ds(me_c, 1), :]
    sin_b = base_ref[1, pl.ds(me_c, 1), :]
    lane = lax.broadcasted_iota(jnp.int32, (rows, 128), 1)
    cosine = cos_b * cos_l - sin_b * sin_l
    sine = sin_b * cos_l + cos_b * sin_l
    sine = jnp.where(lane < 64, -sine, sine)

    span = float(rows)
    lam_full = jnp.exp(-span * rates)
    lam_p0 = jnp.exp(-(span - 1.0) * rates)
    lam_p1 = jnp.exp(-(span - 2.0) * rates)

    def tap(j, p):
        return sf_ref[j, p : p + 1, :]

    def first_rows(p, x0, x1, h0, h1):
        a = tap(0, p) * x0 + tap(1, p) * h1 + tap(2, p) * h0
        b = tap(0, p) * x1 + tap(1, p) * x0 + tap(2, p) * h1
        return a, b

    def first_products(kx, vx, halo):
        k0, k1 = first_rows(1, kx[0], kx[1], halo[2], halo[3])
        v0, v1 = first_rows(2, vx[0], vx[1], halo[4], halo[5])
        return (k0 * v0).astype(BF16).astype(F32), (k1 * v1).astype(BF16).astype(F32)

    def state_step(k, carried):
        total, halo = carried
        pltpu.make_async_remote_copy(
            src_ref=msg,
            dst_ref=msg_in.at[k],
            send_sem=s1.at[0],
            recv_sem=r1.at[k],
            device_id={"ctx": k},
            device_id_type=MESH,
        ).wait_recv()
        got = [msg_in[k, i : i + 1, :] for i in range(16, 26)]
        p0, p1 = first_products(got[6:8], got[8:10], halo)
        total = total * lam_full + msg_in[k, 0:modes, :] + lam_p0 * p0 + lam_p1 * p1
        return total, tuple(got[0:6])

    zero_row = jnp.zeros((1, 128), F32)
    total, halo = lax.fori_loop(
        0, me_c, state_step, (jnp.zeros((modes, 128), F32), (zero_row,) * 6)
    )
    p0, p1 = first_products(
        [xpad[1, 8:9, :], xpad[1, 9:10, :]], [xpad[2, 8:9, :], xpad[2, 9:10, :]], halo
    )
    q0, q1 = first_rows(0, xpad[0, 8:9, :], xpad[0, 9:10, :], halo[0], halo[1])
    total = total * weight
    cross = [jnp.zeros((8, 128), F32) for _ in range(tiles)]
    for m in range(modes):
        e = total[m : m + 1] * jnp.exp(-rates[m : m + 1] * (eight + 1.0))
        for i in range(tiles):
            cross[i] = cross[i] + e
            e = e * lam8[m : m + 1]
    conv = conv + jnp.concatenate(cross, axis=0)
    conv = conv + fsh[0, pl.ds(rows, rows), :] * p0 + fsh[1, pl.ds(rows, rows), :] * p1
    query_part = jnp.where(row_id == 0, q0, jnp.where(row_id == 1, q1, short[0]))
    gated = (query_part * conv).astype(BF16)

    w_copies[0].wait()

    def part_copy(d, target):
        return pltpu.make_async_remote_copy(
            src_ref=part_out.at[d],
            dst_ref=part_in.at[d],
            send_sem=s2.at[d],
            recv_sem=r2.at[d],
            device_id={"tp": target},
            device_id_type=MESH,
        )

    def columns(t):
        return ow[:, pl.ds(pl.multiple_of(t * 128, 128), 128)]

    for d in range(1, n_tp):
        peer = lax.rem(me_t + d, n_tp)
        part_out[d] = jnp.dot(gated, columns(peer), preferred_element_type=F32).astype(BF16)
        part_copy(d, peer).start()
    mix = jnp.dot(gated, columns(me_t), preferred_element_type=F32)
    for d in range(1, n_tp):
        part_copy(d, me_t).wait_recv()
        mix = mix + part_in[d].astype(F32)
    hyena = (resid_ref[...].astype(F32) + mix).astype(BF16)
    gath[me_t] = hyena

    def gath_copy(d, owner, target):
        return pltpu.make_async_remote_copy(
            src_ref=gath.at[owner],
            dst_ref=gath.at[owner],
            send_sem=s3.at[d],
            recv_sem=r3.at[d],
            device_id={"tp": target},
            device_id_type=MESH,
        )

    for d in range(1, n_tp):
        gath_copy(d, me_t, lax.rem(me_t + d, n_tp)).start()
    hy_ref[...] = hyena
    for d in range(1, n_tp):
        gath_copy(d, lax.rem(me_t + n_tp - d, n_tp), me_t).wait_recv()
    wide = [gath[j].astype(F32) for j in range(n_tp)]
    square = wide[0] * wide[0]
    for j in range(1, n_tp):
        square = square + wide[j] * wide[j]
    scale = lax.rsqrt(jnp.sum(square, axis=1, keepdims=True) / float(width) + EPS)
    normed = jnp.concatenate(
        [(wide[j] * scale * gain_ref[j : j + 1, :]).astype(BF16) for j in range(n_tp)], axis=1
    )
    for c in w_copies[1:]:
        c.wait()

    def turned(x):
        return (x * cosine + pltpu.roll(x, 64, axis=1) * sine).astype(BF16)

    key_value = jnp.dot(normed, aw[:, 0:256], preferred_element_type=F32)
    kv[0, me_c] = turned(key_value[:, 0:128])
    kv[1, me_c] = key_value[:, 128:256].astype(BF16)

    def kv_copy(which, d, owner, target):
        return pltpu.make_async_remote_copy(
            src_ref=kv.at[which, owner],
            dst_ref=kv.at[which, owner],
            send_sem=s4.at[which, d],
            recv_sem=r4.at[which, owner],
            device_id={"ctx": target},
            device_id_type=MESH,
        )

    for which in range(2):
        for d in range(1, n_ctx):

            @pl.when(me_c + d < n_ctx)
            def _(which=which, d=d):
                kv_copy(which, d, me_c, me_c + d).start()

    queries = turned(jnp.dot(normed, aw[:, 256:384], preferred_element_type=F32))
    factor = 1.0 / math.sqrt(HEAD_DIM)

    def score_of(k):
        return (
            lax.dot_general(
                queries, kv[0, k], (((1,), (1,)), ((), ())), preferred_element_type=F32
            )
            * factor
        )

    own = jnp.where(row_id >= lane, score_of(me_c), FILL)

    def score_step(k, peak):
        kv_copy(0, 0, k, k).wait_recv()
        s = score_of(k)
        scores[k] = s
        return jnp.maximum(peak, s)

    peak = jnp.max(lax.fori_loop(0, me_c, score_step, own), axis=1, keepdims=True)
    probs = jnp.where(row_id >= lane, jnp.exp(own - peak), 0.0)
    acc = jnp.dot(probs.astype(BF16), kv[1, me_c], preferred_element_type=F32)

    def value_step(k, carried):
        total_p, total_v = carried
        kv_copy(1, 0, k, k).wait_recv()
        pr = jnp.exp(scores[k] - peak)
        total_v = total_v + jnp.dot(pr.astype(BF16), kv[1, k], preferred_element_type=F32)
        return total_p + pr, total_v

    probs, acc = lax.fori_loop(0, me_c, value_step, (probs, acc))
    ctx_ref[...] = (acc / jnp.sum(probs, axis=1, keepdims=True)).astype(BF16)

    for d in range(1, n_tp):
        part_copy(d, me_t).wait_send()
        gath_copy(d, me_t, me_t).wait_send()
    for d in range(1, n_ctx):

        @pl.when(me_c + d < n_ctx)
        def _(d=d):
            msg_copy(d).wait_send()
            kv_copy(0, d, me_c, me_c + d).wait_send()
            kv_copy(1, d, me_c, me_c + d).wait_send()


def rotary_tables(rows, n_ctx):
    half = HEAD_DIM // 2
    freq = ROPE_BASE ** (-np.arange(half, dtype=np.float64) * 2.0 / HEAD_DIM)
    freq = np.concatenate([freq, freq])
    local = np.arange(rows)[:, None] * freq
    base = (np.arange(n_ctx) * rows)[:, None] * freq
    table = np.stack([np.cos(local), np.sin(local)]).astype(np.float32)
    return table, np.stack([np.cos(base), np.sin(base)]).astype(np.float32)


def solution(mesh):
    n_ctx, n_tp = mesh.shape["ctx"], mesh.shape["tp"]

    def per_device(resid, feats, sf, residues, rates, ow, gain, aw):
        rows = resid.shape[0]
        width = ow.shape[1]
        table, base = rotary_tables(rows, n_ctx)
        vmem = pl.BlockSpec(memory_space=pltpu.VMEM)
        hbm = pl.BlockSpec(memory_space=pltpu.HBM)
        dma = pltpu.SemaphoreType.DMA
        block = (rows, 128)
        return pl.pallas_call(
            functools.partial(kernel, n_ctx, n_tp),
            out_shape=(
                pltpu.VMEM(block, BF16),
                pltpu.VMEM(block, BF16),
            ),
            in_specs=[hbm] * 10,
            out_specs=(vmem, vmem),
            scratch_shapes=[
                pltpu.VMEM(block, BF16),
                pltpu.VMEM((3,) + block, BF16),
                pltpu.VMEM(sf.shape, F32),
                pltpu.VMEM(residues.shape[::-1], F32),
                pltpu.VMEM(rates.shape[::-1], F32),
                pltpu.VMEM((n_tp, 128), F32),
                pltpu.VMEM(table.shape, F32),
                pltpu.VMEM(base.shape, F32),
                pltpu.VMEM(ow.shape, BF16),
                pltpu.VMEM((width, 384), BF16),
                pltpu.VMEM((3, rows + 8, 128), F32),
                pltpu.VMEM(block, F32),
                pltpu.VMEM((8, 2 * rows, 128), F32),
                pltpu.VMEM((32, 128), F32),
                pltpu.VMEM((n_ctx, 32, 128), F32),
                pltpu.VMEM((n_tp,) + block, BF16),
                pltpu.VMEM((n_tp,) + block, BF16),
                pltpu.VMEM((n_tp,) + block, BF16),
                pltpu.VMEM((2, n_ctx) + block, BF16),
                pltpu.VMEM((n_ctx,) + block, F32),
                dma((4,)),
                dma((8,)),
                dma((n_ctx,)),
                dma((n_ctx,)),
                dma((n_tp,)),
                dma((n_tp,)),
                dma((n_tp,)),
                dma((n_tp,)),
                dma((2, n_ctx)),
                dma((2, n_ctx)),
            ],
            compiler_params=pltpu.CompilerParams(
                collective_id=0, has_side_effects=True, vmem_limit_bytes=56 * 1024 * 1024
            ),
        )(
            resid,
            feats.transpose(1, 0, 2),
            sf,
            residues.T,
            rates.T,
            gain.reshape(n_tp, 128),
            jnp.asarray(table),
            jnp.asarray(base),
            ow,
            aw.transpose(1, 0, 2),
        )

    in_specs = (
        P("ctx", "tp"),
        P("ctx", None, "tp"),
        P(None, None, "tp"),
        P("tp", None),
        P("tp", None),
        P("tp", None),
        P(),
        P(None, None, "tp"),
    )
    return jax.shard_map(
        per_device,
        mesh=mesh,
        in_specs=in_specs,
        out_specs=(P("ctx", "tp"), P("ctx", "tp")),
        check_vma=False,
    )
```

```python
import functools
import math

import jax
import jax.numpy as jnp
import numpy as np
from jax import lax
from jax.experimental import pallas as pl
from jax.experimental.pallas import tpu as pltpu
from jax.sharding import PartitionSpec as P

HEAD_DIM = 128
EPS = 1e-05
ROPE_BASE = 10000.0
FILL = -1e30
MESH = pl.DeviceIdType.MESH
F32 = jnp.float32
BF16 = jnp.bfloat16


def kernel(
    n_ctx,
    n_tp,
    resid_hbm,
    feats_hbm,
    sf_hbm,
    res_hbm,
    rate_hbm,
    gain_hbm,
    table_hbm,
    base_hbm,
    ow_hbm,
    aw_hbm,
    hy_ref,
    ctx_ref,
    resid_ref,
    feats_ref,
    sf_ref,
    res_ref,
    rate_ref,
    gain_ref,
    table_ref,
    base_ref,
    ow,
    aw,
    xpad,
    prod,
    fsh,
    msg,
    msg_in,
    pair_out,
    pair_in,
    part_out,
    part_in,
    gath,
    kv,
    scores,
    w_sem,
    in_sem,
    s1,
    r1,
    s2,
    r2,
    s3,
    r3,
    s4,
    r4,
    s5,
    r5,
):
    me_c = lax.axis_index("ctx")
    me_t = lax.axis_index("tp")
    rows = resid_ref.shape[0]
    modes = res_ref.shape[0]
    width = n_tp * 128
    tiles = rows // 8
    n_chip = n_tp // 2
    core = lax.rem(me_t, 2)
    chip = me_t // 2
    partner = chip * 2 + 1 - core

    def same_core(d):
        return lax.rem(chip + d, n_chip) * 2 + core

    in_copies = []
    for i, (src, dst) in enumerate(
        (
            (feats_hbm, feats_ref),
            (sf_hbm, sf_ref),
            (rate_hbm, rate_ref),
            (res_hbm, res_ref),
            (table_hbm, table_ref),
            (base_hbm, base_ref),
            (resid_hbm, resid_ref),
            (gain_hbm, gain_ref),
        )
    ):
        in_copies.append(pltpu.make_async_copy(src, dst, in_sem.at[i]))
    for c in in_copies:
        c.start()

    barrier = pltpu.get_barrier_semaphore()
    for peer in [partner] + [same_core(d) for d in range(1, n_chip)]:
        pl.semaphore_signal(barrier, inc=1, device_id={"tp": peer}, device_id_type=MESH)
    for d in range(1, n_ctx):

        @pl.when(me_c >= d)
        def _(d=d):
            pl.semaphore_signal(
                barrier, inc=1, device_id={"ctx": me_c - d}, device_id_type=MESH
            )

    w_copies = [pltpu.make_async_copy(ow_hbm, ow, w_sem.at[0])]
    for slot, p in enumerate((1, 2, 0)):
        w_copies.append(
            pltpu.make_async_copy(
                aw_hbm.at[p], aw.at[:, pl.ds(slot * 128, 128)], w_sem.at[1 + slot]
            )
        )
    for c in w_copies:
        c.start()

    for c in in_copies[0:3]:
        c.wait()

    short = []
    for p in range(3):
        x = feats_ref[p].astype(F32)
        xpad[p, 0:8, :] = jnp.zeros((8, 128), F32)
        xpad[p, pl.ds(8, rows), :] = x
        short.append(
            sf_ref[0, p : p + 1, :] * x
            + sf_ref[1, p : p + 1, :] * xpad[p, pl.ds(7, rows), :]
            + sf_ref[2, p : p + 1, :] * xpad[p, pl.ds(6, rows), :]
        )
    row_id = lax.broadcasted_iota(jnp.int32, (rows, 128), 0)
    p_mask = jnp.where(row_id >= 2, (short[1] * short[2]).astype(BF16).astype(F32), 0.0)
    prod[...] = p_mask

    rates = rate_ref[...]
    eight = lax.broadcasted_iota(jnp.int32, (8, 128), 0).astype(F32)
    lam8 = jnp.exp(-8.0 * rates)

    for m in range(modes):
        state = p_mask[0:8]
        for i in range(1, tiles):
            state = state * lam8[m : m + 1] + p_mask[8 * i : 8 * i + 8]
        state = state * jnp.exp(-rates[m : m + 1] * (7.0 - eight))
        msg[m : m + 1, :] = jnp.sum(state, axis=0, keepdims=True)
    for p in range(3):
        msg[16 + 2 * p : 18 + 2 * p, :] = xpad[p, rows + 6 : rows + 8, :]
    for p in range(1, 3):
        msg[20 + 2 * p : 22 + 2 * p, :] = xpad[p, 8:10, :]
    msg[26:32, :] = jnp.zeros((6, 128), F32)

    pl.semaphore_wait(barrier, n_chip + (n_ctx - 1 - me_c))

    def msg_copy(d):
        return pltpu.make_async_remote_copy(
            src_ref=msg,
            dst_ref=msg_in.at[me_c],
            send_sem=s1.at[d],
            recv_sem=r1.at[me_c],
            device_id={"ctx": me_c + d},
            device_id_type=MESH,
        )

    for d in range(1, n_ctx):

        @pl.when(me_c + d < n_ctx)
        def _(d=d):
            msg_copy(d).start()

    for c in in_copies[3:]:
        c.wait()
    weight = res_ref[...] * jnp.sqrt(1.0 - jnp.exp(-2.0 * rates))
    taps = [jnp.zeros((8, 128), F32) for _ in range(tiles)]
    for m in range(modes):
        e = weight[m : m + 1] * jnp.exp(-rates[m : m + 1] * eight)
        for i in range(tiles):
            taps[i] = taps[i] + e
            e = e * lam8[m : m + 1]
    taps = jnp.concatenate(taps, axis=0)
    for r in range(8):
        fsh[r, 0 : rows + 8, :] = jnp.zeros((rows + 8, 128), F32)
        fsh[r, rows + r : 2 * rows, :] = taps[0 : rows - r]

    def conv_step(j, acc):
        start = pl.multiple_of(rows - 8 * j, 8)
        block = prod[pl.ds(pl.multiple_of(8 * j, 8), 8), :]
        for r in range(8):
            acc = acc + fsh[r, pl.ds(start, rows), :] * block[r : r + 1]
        return acc

    conv = lax.fori_loop(0, tiles, conv_step, jnp.zeros((rows, 128), F32))

    cos_l, sin_l = table_ref[0], table_ref[1]
    cos_b = base_ref[0, pl.ds(me_c, 1), :]
    sin_b = base_ref[1, pl.ds(me_c, 1), :]
    lane = lax.broadcasted_iota(jnp.int32, (rows, 128), 1)
    cosine = cos_b * cos_l - sin_b * sin_l
    sine = sin_b * cos_l + cos_b * sin_l
    sine = jnp.where(lane < 64, -sine, sine)

    span = float(rows)
    lam_full = jnp.exp(-span * rates)
    lam_p0 = jnp.exp(-(span - 1.0) * rates)
    lam_p1 = jnp.exp(-(span - 2.0) * rates)

    def tap(j, p):
        return sf_ref[j, p : p + 1, :]

    def first_rows(p, x0, x1, h0, h1):
        a = tap(0, p) * x0 + tap(1, p) * h1 + tap(2, p) * h0
        b = tap(0, p) * x1 + tap(1, p) * x0 + tap(2, p) * h1
        return a, b

    def first_products(kx, vx, halo):
        k0, k1 = first_rows(1, kx[0], kx[1], halo[2], halo[3])
        v0, v1 = first_rows(2, vx[0], vx[1], halo[4], halo[5])
        return (k0 * v0).astype(BF16).astype(F32), (k1 * v1).astype(BF16).astype(F32)

    def state_step(k, carried):
        total, halo = carried
        pltpu.make_async_remote_copy(
            src_ref=msg,
            dst_ref=msg_in.at[k],
            send_sem=s1.at[0],
            recv_sem=r1.at[k],
            device_id={"ctx": k},
            device_id_type=MESH,
        ).wait_recv()
        got = [msg_in[k, i : i + 1, :] for i in range(16, 26)]
        p0, p1 = first_products(got[6:8], got[8:10], halo)
        total = total * lam_full + msg_in[k, 0:modes, :] + lam_p0 * p0 + lam_p1 * p1
        return total, tuple(got[0:6])

    zero_row = jnp.zeros((1, 128), F32)
    total, halo = lax.fori_loop(
        0, me_c, state_step, (jnp.zeros((modes, 128), F32), (zero_row,) * 6)
    )
    p0, p1 = first_products(
        [xpad[1, 8:9, :], xpad[1, 9:10, :]], [xpad[2, 8:9, :], xpad[2, 9:10, :]], halo
    )
    q0, q1 = first_rows(0, xpad[0, 8:9, :], xpad[0, 9:10, :], halo[0], halo[1])
    total = total * weight
    cross = [jnp.zeros((8, 128), F32) for _ in range(tiles)]
    for m in range(modes):
        e = total[m : m + 1] * jnp.exp(-rates[m : m + 1] * (eight + 1.0))
        for i in range(tiles):
            cross[i] = cross[i] + e
            e = e * lam8[m : m + 1]
    conv = conv + jnp.concatenate(cross, axis=0)
    conv = conv + fsh[0, pl.ds(rows, rows), :] * p0 + fsh[1, pl.ds(rows, rows), :] * p1
    query_part = jnp.where(row_id == 0, q0, jnp.where(row_id == 1, q1, short[0]))
    gated = (query_part * conv).astype(BF16)

    w_copies[0].wait()

    def pair_copy(d):
        return pltpu.make_async_remote_copy(
            src_ref=pair_out.at[d],
            dst_ref=pair_in.at[d],
            send_sem=s5.at[d],
            recv_sem=r5.at[d],
            device_id={"tp": partner},
            device_id_type=MESH,
        )

    def part_copy(d):
        return pltpu.make_async_remote_copy(
            src_ref=part_out.at[d],
            dst_ref=part_in.at[d],
            send_sem=s2.at[d],
            recv_sem=r2.at[d],
            device_id={"tp": same_core(d)},
            device_id_type=MESH,
        )

    def share(t):
        cols = ow[:, pl.ds(pl.multiple_of(t * 128, 128), 128)]
        return jnp.dot(gated, cols, preferred_element_type=F32)

    order = list(range(1, n_chip)) + [0]
    for d in order:
        pair_out[d] = share(lax.rem(chip + d, n_chip) * 2 + 1 - core)
        pair_copy(d).start()
    mine = [share(same_core(d)) for d in order]
    for d in range(1, n_chip):
        pair_copy(d).wait_recv()
        part_out[d] = (mine[d - 1] + pair_in[d]).astype(BF16)
        part_copy(d).start()
    pair_copy(0).wait_recv()
    mix = resid_ref[...].astype(F32) + (mine[-1] + pair_in[0])
    for d in range(1, n_chip):
        part_copy(d).wait_recv()
        mix = mix + part_in[d].astype(F32)
    hyena = mix.astype(BF16)
    gath[me_t] = hyena

    def gath_copy(sem, owner, target):
        return pltpu.make_async_remote_copy(
            src_ref=gath.at[owner],
            dst_ref=gath.at[owner],
            send_sem=s3.at[sem],
            recv_sem=r3.at[owner],
            device_id={"tp": target},
            device_id_type=MESH,
        )

    for d in range(1, n_chip):
        gath_copy(d, me_t, same_core(d)).start()
    gath_copy(0, me_t, partner).start()
    hy_ref[...] = hyena
    wide = hyena.astype(F32)
    square = wide * wide
    gath_copy(0, partner, partner).wait_recv()
    wide = gath[partner].astype(F32)
    square = square + wide * wide
    for d in range(1, n_chip):
        owner = same_core(n_chip - d)
        gath_copy(d, owner, partner).wait_recv()
        gath_copy(n_chip + d, owner, partner).start()
        wide = gath[owner].astype(F32)
        square = square + wide * wide
    for d in range(1, n_chip):
        owner = lax.rem(chip + n_chip - d, n_chip) * 2 + 1 - core
        gath_copy(d, owner, partner).wait_recv()
        wide = gath[owner].astype(F32)
        square = square + wide * wide
    scale = lax.rsqrt(jnp.sum(square, axis=1, keepdims=True) / float(width) + EPS)
    normed = jnp.concatenate(
        [(gath[j].astype(F32) * scale * gain_ref[j : j + 1, :]).astype(BF16) for j in range(n_tp)], axis=1
    )
    for c in w_copies[1:]:
        c.wait()

    def turned(x):
        return (x * cosine + pltpu.roll(x, 64, axis=1) * sine).astype(BF16)

    key_value = jnp.dot(normed, aw[:, 0:256], preferred_element_type=F32)
    kv[0, me_c] = turned(key_value[:, 0:128])
    kv[1, me_c] = key_value[:, 128:256].astype(BF16)

    def kv_copy(which, d, owner, target):
        return pltpu.make_async_remote_copy(
            src_ref=kv.at[which, owner],
            dst_ref=kv.at[which, owner],
            send_sem=s4.at[which, d],
            recv_sem=r4.at[which, owner],
            device_id={"ctx": target},
            device_id_type=MESH,
        )

    for which in range(2):
        for d in range(1, n_ctx):

            @pl.when(me_c + d < n_ctx)
            def _(which=which, d=d):
                kv_copy(which, d, me_c, me_c + d).start()

    queries = turned(jnp.dot(normed, aw[:, 256:384], preferred_element_type=F32))
    factor = 1.0 / math.sqrt(HEAD_DIM)

    def score_of(k):
        return (
            lax.dot_general(
                queries, kv[0, k], (((1,), (1,)), ((), ())), preferred_element_type=F32
            )
            * factor
        )

    own = jnp.where(row_id >= lane, score_of(me_c), FILL)

    def score_step(k, peak):
        kv_copy(0, 0, k, k).wait_recv()
        s = score_of(k)
        scores[k] = s
        return jnp.maximum(peak, s)

    peak = jnp.max(lax.fori_loop(0, me_c, score_step, own), axis=1, keepdims=True)
    probs = jnp.where(row_id >= lane, jnp.exp(own - peak), 0.0)
    acc = jnp.dot(probs.astype(BF16), kv[1, me_c], preferred_element_type=F32)

    def value_step(k, carried):
        total_p, total_v = carried
        kv_copy(1, 0, k, k).wait_recv()
        pr = jnp.exp(scores[k] - peak)
        total_v = total_v + jnp.dot(pr.astype(BF16), kv[1, k], preferred_element_type=F32)
        return total_p + pr, total_v

    probs, acc = lax.fori_loop(0, me_c, value_step, (probs, acc))
    ctx_ref[...] = (acc / jnp.sum(probs, axis=1, keepdims=True)).astype(BF16)

    for d in range(n_chip):
        pair_copy(d).wait_send()
        gath_copy(d, me_t, partner).wait_send()
        if d > 0:
            part_copy(d).wait_send()
            gath_copy(n_chip + d, me_t, partner).wait_send()
    for d in range(1, n_ctx):

        @pl.when(me_c + d < n_ctx)
        def _(d=d):
            msg_copy(d).wait_send()
            kv_copy(0, d, me_c, me_c + d).wait_send()
            kv_copy(1, d, me_c, me_c + d).wait_send()


def rotary_tables(rows, n_ctx):
    half = HEAD_DIM // 2
    freq = ROPE_BASE ** (-np.arange(half, dtype=np.float64) * 2.0 / HEAD_DIM)
    freq = np.concatenate([freq, freq])
    local = np.arange(rows)[:, None] * freq
    base = (np.arange(n_ctx) * rows)[:, None] * freq
    table = np.stack([np.cos(local), np.sin(local)]).astype(np.float32)
    return table, np.stack([np.cos(base), np.sin(base)]).astype(np.float32)


def solution(mesh):
    n_ctx, n_tp = mesh.shape["ctx"], mesh.shape["tp"]

    def per_device(resid, feats, sf, residues, rates, ow, gain, aw):
        rows = resid.shape[0]
        width = ow.shape[1]
        table, base = rotary_tables(rows, n_ctx)
        vmem = pl.BlockSpec(memory_space=pltpu.VMEM)
        hbm = pl.BlockSpec(memory_space=pltpu.HBM)
        dma = pltpu.SemaphoreType.DMA
        block = (rows, 128)
        return pl.pallas_call(
            functools.partial(kernel, n_ctx, n_tp),
            out_shape=(
                pltpu.VMEM(block, BF16),
                pltpu.VMEM(block, BF16),
            ),
            in_specs=[hbm] * 10,
            out_specs=(vmem, vmem),
            scratch_shapes=[
                pltpu.VMEM(block, BF16),
                pltpu.VMEM((3,) + block, BF16),
                pltpu.VMEM(sf.shape, F32),
                pltpu.VMEM(residues.shape[::-1], F32),
                pltpu.VMEM(rates.shape[::-1], F32),
                pltpu.VMEM((n_tp, 128), F32),
                pltpu.VMEM(table.shape, F32),
                pltpu.VMEM(base.shape, F32),
                pltpu.VMEM(ow.shape, BF16),
                pltpu.VMEM((width, 384), BF16),
                pltpu.VMEM((3, rows + 8, 128), F32),
                pltpu.VMEM(block, F32),
                pltpu.VMEM((8, 2 * rows, 128), F32),
                pltpu.VMEM((32, 128), F32),
                pltpu.VMEM((n_ctx, 32, 128), F32),
                pltpu.VMEM((n_tp // 2,) + block, F32),
                pltpu.VMEM((n_tp // 2,) + block, F32),
                pltpu.VMEM((n_tp // 2,) + block, BF16),
                pltpu.VMEM((n_tp // 2,) + block, BF16),
                pltpu.VMEM((n_tp,) + block, BF16),
                pltpu.VMEM((2, n_ctx) + block, BF16),
                pltpu.VMEM((n_ctx,) + block, F32),
                dma((4,)),
                dma((8,)),
                dma((n_ctx,)),
                dma((n_ctx,)),
                dma((n_tp,)),
                dma((n_tp,)),
                dma((n_tp,)),
                dma((n_tp,)),
                dma((2, n_ctx)),
                dma((2, n_ctx)),
                dma((n_tp // 2,)),
                dma((n_tp // 2,)),
            ],
            compiler_params=pltpu.CompilerParams(
                collective_id=0, has_side_effects=True, vmem_limit_bytes=56 * 1024 * 1024
            ),
        )(
            resid,
            feats.transpose(1, 0, 2),
            sf,
            residues.T,
            rates.T,
            gain.reshape(n_tp, 128),
            jnp.asarray(table),
            jnp.asarray(base),
            ow,
            aw.transpose(1, 0, 2),
        )

    in_specs = (
        P("ctx", "tp"),
        P("ctx", None, "tp"),
        P(None, None, "tp"),
        P("tp", None),
        P("tp", None),
        P("tp", None),
        P(),
        P(None, None, "tp"),
    )
    return jax.shard_map(
        per_device,
        mesh=mesh,
        in_specs=in_specs,
        out_specs=(P("ctx", "tp"), P("ctx", "tp")),
        check_vma=False,
    )
```

```python
import functools
import math

import jax
import jax.numpy as jnp
import numpy as np
from jax import lax
from jax.experimental import pallas as pl
from jax.experimental.pallas import tpu as pltpu
from jax.sharding import PartitionSpec as P

HEAD_DIM = 128
EPS = 1e-05
ROPE_BASE = 10000.0
FILL = -1e30
MESH = pl.DeviceIdType.MESH
F32 = jnp.float32
BF16 = jnp.bfloat16


def kernel(
    n_ctx,
    n_tp,
    resid_hbm,
    feats_hbm,
    sf_hbm,
    res_hbm,
    rate_hbm,
    gain_hbm,
    table_hbm,
    base_hbm,
    ow_hbm,
    aw_hbm,
    hy_ref,
    ctx_ref,
    resid_ref,
    feats_ref,
    sf_ref,
    res_ref,
    rate_ref,
    gain_ref,
    table_ref,
    base_ref,
    ow,
    aw,
    xpad,
    prod,
    fsh,
    msg,
    msg_in,
    pair_out,
    pair_in,
    part_out,
    part_in,
    gath,
    kv,
    w_sem,
    in_sem,
    s1,
    r1,
    s2,
    r2,
    s3,
    r3,
    s4,
    r4,
    s5,
    r5,
):
    me_c = lax.axis_index("ctx")
    me_t = lax.axis_index("tp")
    rows = resid_ref.shape[0]
    modes = res_ref.shape[0]
    width = n_tp * 128
    tiles = rows // 8
    n_chip = n_tp // 2
    core = lax.rem(me_t, 2)
    chip = me_t // 2
    partner = chip * 2 + 1 - core

    def same_core(d):
        return lax.rem(chip + d, n_chip) * 2 + core

    in_copies = []
    for i, (src, dst) in enumerate(
        (
            (feats_hbm, feats_ref),
            (sf_hbm, sf_ref),
            (rate_hbm, rate_ref),
            (res_hbm, res_ref),
            (table_hbm, table_ref),
            (base_hbm, base_ref),
            (resid_hbm, resid_ref),
            (gain_hbm, gain_ref),
        )
    ):
        in_copies.append(pltpu.make_async_copy(src, dst, in_sem.at[i]))
    for c in in_copies:
        c.start()

    barrier = pltpu.get_barrier_semaphore()
    for peer in [partner] + [same_core(d) for d in range(1, n_chip)]:
        pl.semaphore_signal(barrier, inc=1, device_id={"tp": peer}, device_id_type=MESH)
    for d in range(1, n_ctx):

        @pl.when(me_c >= d)
        def _(d=d):
            pl.semaphore_signal(
                barrier, inc=1, device_id={"ctx": me_c - d}, device_id_type=MESH
            )

    w_copies = [pltpu.make_async_copy(ow_hbm, ow, w_sem.at[0])]
    for slot, p in enumerate((1, 2, 0)):
        w_copies.append(
            pltpu.make_async_copy(
                aw_hbm.at[p], aw.at[:, pl.ds(slot * 128, 128)], w_sem.at[1 + slot]
            )
        )
    for c in w_copies:
        c.start()

    for c in in_copies[0:3]:
        c.wait()

    short = []
    for p in range(3):
        x = feats_ref[p].astype(F32)
        xpad[p, 0:8, :] = jnp.zeros((8, 128), F32)
        xpad[p, pl.ds(8, rows), :] = x
        short.append(
            sf_ref[0, p : p + 1, :] * x
            + sf_ref[1, p : p + 1, :] * xpad[p, pl.ds(7, rows), :]
            + sf_ref[2, p : p + 1, :] * xpad[p, pl.ds(6, rows), :]
        )
    row_id = lax.broadcasted_iota(jnp.int32, (rows, 128), 0)
    p_mask = jnp.where(row_id >= 2, (short[1] * short[2]).astype(BF16).astype(F32), 0.0)
    prod[...] = p_mask

    rates = rate_ref[...]
    eight = lax.broadcasted_iota(jnp.int32, (8, 128), 0).astype(F32)
    lam8 = jnp.exp(-8.0 * rates)

    for m in range(modes):
        state = p_mask[0:8]
        for i in range(1, tiles):
            state = state * lam8[m : m + 1] + p_mask[8 * i : 8 * i + 8]
        state = state * jnp.exp(-rates[m : m + 1] * (7.0 - eight))
        msg[m : m + 1, :] = jnp.sum(state, axis=0, keepdims=True)
    for p in range(3):
        msg[16 + 2 * p : 18 + 2 * p, :] = xpad[p, rows + 6 : rows + 8, :]
    for p in range(1, 3):
        msg[20 + 2 * p : 22 + 2 * p, :] = xpad[p, 8:10, :]
    msg[26:32, :] = jnp.zeros((6, 128), F32)

    pl.semaphore_wait(barrier, n_chip + (n_ctx - 1 - me_c))

    def msg_copy(d):
        return pltpu.make_async_remote_copy(
            src_ref=msg,
            dst_ref=msg_in.at[me_c],
            send_sem=s1.at[d],
            recv_sem=r1.at[me_c],
            device_id={"ctx": me_c + d},
            device_id_type=MESH,
        )

    for d in range(1, n_ctx):

        @pl.when(me_c + d < n_ctx)
        def _(d=d):
            msg_copy(d).start()

    for c in in_copies[3:]:
        c.wait()
    weight = res_ref[...] * jnp.sqrt(1.0 - jnp.exp(-2.0 * rates))
    taps = [jnp.zeros((8, 128), F32) for _ in range(tiles)]
    for m in range(modes):
        e = weight[m : m + 1] * jnp.exp(-rates[m : m + 1] * eight)
        for i in range(tiles):
            taps[i] = taps[i] + e
            e = e * lam8[m : m + 1]
    taps = jnp.concatenate(taps, axis=0)
    for r in range(8):
        fsh[r, 0 : rows + 8, :] = jnp.zeros((rows + 8, 128), F32)
        fsh[r, rows + r : 2 * rows, :] = taps[0 : rows - r]

    def conv_step(j, acc):
        start = pl.multiple_of(rows - 8 * j, 8)
        block = prod[pl.ds(pl.multiple_of(8 * j, 8), 8), :]
        for r in range(8):
            acc = acc + fsh[r, pl.ds(start, rows), :] * block[r : r + 1]
        return acc

    def conv_step_low(j, acc):
        start = pl.multiple_of(rows + rows // 2 - 8 * j, 8)
        block = prod[pl.ds(pl.multiple_of(8 * j, 8), 8), :]
        for r in range(8):
            acc = acc + fsh[r, pl.ds(start, rows // 2), :] * block[r : r + 1]
        return acc

    conv = lax.fori_loop(0, tiles // 2, conv_step, jnp.zeros((rows, 128), F32))
    low = lax.fori_loop(tiles // 2, tiles, conv_step_low, conv[rows // 2 :])
    conv = jnp.concatenate([conv[: rows // 2], low], axis=0)

    for k in range(1, n_ctx):

        @pl.when(k > me_c)
        def _(k=k):
            kv[0, k] = jnp.zeros((rows, 128), BF16)
            kv[1, k] = jnp.zeros((rows, 128), BF16)

    cos_l, sin_l = table_ref[0], table_ref[1]
    cos_b = base_ref[0, pl.ds(me_c, 1), :]
    sin_b = base_ref[1, pl.ds(me_c, 1), :]
    lane = lax.broadcasted_iota(jnp.int32, (rows, 128), 1)
    cosine = cos_b * cos_l - sin_b * sin_l
    sine = sin_b * cos_l + cos_b * sin_l
    sine = jnp.where(lane < 64, -sine, sine)

    span = float(rows)
    lam_full = jnp.exp(-span * rates)
    lam_p0 = jnp.exp(-(span - 1.0) * rates)
    lam_p1 = jnp.exp(-(span - 2.0) * rates)

    def tap(j, p):
        return sf_ref[j, p : p + 1, :]

    def first_rows(p, x0, x1, h0, h1):
        a = tap(0, p) * x0 + tap(1, p) * h1 + tap(2, p) * h0
        b = tap(0, p) * x1 + tap(1, p) * x0 + tap(2, p) * h1
        return a, b

    def first_products(kx, vx, halo):
        k0, k1 = first_rows(1, kx[0], kx[1], halo[2], halo[3])
        v0, v1 = first_rows(2, vx[0], vx[1], halo[4], halo[5])
        return (k0 * v0).astype(BF16).astype(F32), (k1 * v1).astype(BF16).astype(F32)

    def state_step(k, carried):
        total, halo = carried
        pltpu.make_async_remote_copy(
            src_ref=msg,
            dst_ref=msg_in.at[k],
            send_sem=s1.at[0],
            recv_sem=r1.at[k],
            device_id={"ctx": k},
            device_id_type=MESH,
        ).wait_recv()
        got = [msg_in[k, i : i + 1, :] for i in range(16, 26)]
        p0, p1 = first_products(got[6:8], got[8:10], halo)
        total = total * lam_full + msg_in[k, 0:modes, :] + lam_p0 * p0 + lam_p1 * p1
        return total, tuple(got[0:6])

    zero_row = jnp.zeros((1, 128), F32)
    total, halo = lax.fori_loop(
        0, me_c, state_step, (jnp.zeros((modes, 128), F32), (zero_row,) * 6)
    )
    p0, p1 = first_products(
        [xpad[1, 8:9, :], xpad[1, 9:10, :]], [xpad[2, 8:9, :], xpad[2, 9:10, :]], halo
    )
    q0, q1 = first_rows(0, xpad[0, 8:9, :], xpad[0, 9:10, :], halo[0], halo[1])
    total = total * weight
    cross = [jnp.zeros((8, 128), F32) for _ in range(tiles)]
    for m in range(modes):
        e = total[m : m + 1] * jnp.exp(-rates[m : m + 1] * (eight + 1.0))
        for i in range(tiles):
            cross[i] = cross[i] + e
            e = e * lam8[m : m + 1]
    conv = conv + jnp.concatenate(cross, axis=0)
    conv = conv + fsh[0, pl.ds(rows, rows), :] * p0 + fsh[1, pl.ds(rows, rows), :] * p1
    query_part = jnp.where(row_id == 0, q0, jnp.where(row_id == 1, q1, short[0]))
    gated = (query_part * conv).astype(BF16)

    w_copies[0].wait()

    def pair_copy(d):
        return pltpu.make_async_remote_copy(
            src_ref=pair_out.at[d],
            dst_ref=pair_in.at[d],
            send_sem=s5.at[d],
            recv_sem=r5.at[d],
            device_id={"tp": partner},
            device_id_type=MESH,
        )

    def part_copy(d):
        return pltpu.make_async_remote_copy(
            src_ref=part_out.at[d],
            dst_ref=part_in.at[d],
            send_sem=s2.at[d],
            recv_sem=r2.at[d],
            device_id={"tp": same_core(d)},
            device_id_type=MESH,
        )

    mine = [None] * n_chip
    for d in list(range(1, n_chip)) + [0]:
        start = pl.multiple_of(lax.rem(chip + d, n_chip) * 256, 256)
        both = jnp.dot(gated, ow[:, pl.ds(start, 256)], preferred_element_type=F32)
        pair_out[d] = jnp.where(core == 0, both[:, 128:256], both[:, 0:128])
        pair_copy(d).start()
        mine[d] = jnp.where(core == 0, both[:, 0:128], both[:, 128:256])
    for d in range(1, n_chip):
        pair_copy(d).wait_recv()
        part_out[d] = (mine[d] + pair_in[d]).astype(BF16)
        part_copy(d).start()
    pair_copy(0).wait_recv()
    mix = resid_ref[...].astype(F32) + (mine[0] + pair_in[0])
    for d in range(1, n_chip):
        part_copy(d).wait_recv()
        mix = mix + part_in[d].astype(F32)
    hyena = mix.astype(BF16)
    gath[me_t] = hyena

    def gath_copy(sem, owner, target):
        return pltpu.make_async_remote_copy(
            src_ref=gath.at[owner],
            dst_ref=gath.at[owner],
            send_sem=s3.at[sem],
            recv_sem=r3.at[owner],
            device_id={"tp": target},
            device_id_type=MESH,
        )

    for d in range(1, n_chip):
        gath_copy(d, me_t, same_core(d)).start()
    gath_copy(0, me_t, partner).start()
    hy_ref[...] = hyena
    for c in w_copies[1:]:
        c.wait()

    def chip_block(t, square, key_value, query):
        scaled = []
        for i in range(2):
            wide = gath[2 * t + i].astype(F32)
            square = square + wide * wide
            scaled.append((wide * gain_ref[pl.ds(2 * t + i, 1), :]).astype(BF16))
        scaled = jnp.concatenate(scaled, axis=1)
        weights = pl.ds(pl.multiple_of(t * 256, 256), 256)
        key_value = key_value + jnp.dot(scaled, aw[weights, 0:256], preferred_element_type=F32)
        query = query + jnp.dot(scaled, aw[weights, 256:384], preferred_element_type=F32)
        return square, key_value, query

    gath_copy(0, partner, partner).wait_recv()
    sums = chip_block(
        chip,
        jnp.zeros((rows, 128), F32),
        jnp.zeros((rows, 256), F32),
        jnp.zeros((rows, 128), F32),
    )
    for d in range(1, n_chip):
        owner = same_core(n_chip - d)
        gath_copy(d, owner, partner).wait_recv()
        gath_copy(n_chip + d, owner, partner).start()
    for d in range(1, n_chip):
        source = lax.rem(chip + n_chip - d, n_chip)
        gath_copy(d, source * 2 + 1 - core, partner).wait_recv()
        sums = chip_block(source, *sums)
    square, key_value, query = sums
    scale = lax.rsqrt(jnp.sum(square, axis=1, keepdims=True) / float(width) + EPS)

    def turned(x):
        return (x * cosine + pltpu.roll(x, 64, axis=1) * sine).astype(BF16)

    kv[0, me_c] = turned(key_value[:, 0:128] * scale)
    kv[1, me_c] = (key_value[:, 128:256] * scale).astype(BF16)

    def kv_copy(which, d, owner, target):
        return pltpu.make_async_remote_copy(
            src_ref=kv.at[which, owner],
            dst_ref=kv.at[which, owner],
            send_sem=s4.at[which, d],
            recv_sem=r4.at[which, owner],
            device_id={"ctx": target},
            device_id_type=MESH,
        )

    for which in range(2):
        for d in range(1, n_ctx):

            @pl.when(me_c + d < n_ctx)
            def _(which=which, d=d):
                kv_copy(which, d, me_c, me_c + d).start()

    queries = turned(query * scale)
    factor = 1.0 / math.sqrt(HEAD_DIM)
    keys_n = n_ctx * rows

    def arrived(which):
        for k in range(n_ctx - 1):

            @pl.when(k < me_c)
            def _(k=k):
                kv_copy(which, 0, k, k).wait_recv()

    row_pos = me_c * rows + lax.broadcasted_iota(jnp.int32, (rows, keys_n), 0)
    allowed = row_pos >= lax.broadcasted_iota(jnp.int32, (rows, keys_n), 1)
    arrived(0)
    scores = (
        lax.dot_general(
            queries,
            kv[0].reshape(keys_n, 128),
            (((1,), (1,)), ((), ())),
            preferred_element_type=F32,
        )
        * factor
    )
    scores = jnp.where(allowed, scores, FILL)
    probs = jnp.exp(scores - jnp.max(scores, axis=1, keepdims=True))
    probs = jnp.where(allowed, probs, 0.0)
    total_p = jnp.sum(probs, axis=1, keepdims=True)
    arrived(1)
    acc = jnp.dot(
        probs.astype(BF16), kv[1].reshape(keys_n, 128), preferred_element_type=F32
    )
    ctx_ref[...] = (acc / total_p).astype(BF16)

    for d in range(n_chip):
        pair_copy(d).wait_send()
        gath_copy(d, me_t, partner).wait_send()
        if d > 0:
            part_copy(d).wait_send()
            gath_copy(n_chip + d, me_t, partner).wait_send()
    for d in range(1, n_ctx):

        @pl.when(me_c + d < n_ctx)
        def _(d=d):
            msg_copy(d).wait_send()
            kv_copy(0, d, me_c, me_c + d).wait_send()
            kv_copy(1, d, me_c, me_c + d).wait_send()


def rotary_tables(rows, n_ctx):
    half = HEAD_DIM // 2
    freq = ROPE_BASE ** (-np.arange(half, dtype=np.float64) * 2.0 / HEAD_DIM)
    freq = np.concatenate([freq, freq])
    local = np.arange(rows)[:, None] * freq
    base = (np.arange(n_ctx) * rows)[:, None] * freq
    table = np.stack([np.cos(local), np.sin(local)]).astype(np.float32)
    return table, np.stack([np.cos(base), np.sin(base)]).astype(np.float32)


def solution(mesh):
    n_ctx, n_tp = mesh.shape["ctx"], mesh.shape["tp"]

    def per_device(resid, feats, sf, residues, rates, ow, gain, aw):
        rows = resid.shape[0]
        width = ow.shape[1]
        table, base = rotary_tables(rows, n_ctx)
        vmem = pl.BlockSpec(memory_space=pltpu.VMEM)
        hbm = pl.BlockSpec(memory_space=pltpu.HBM)
        dma = pltpu.SemaphoreType.DMA
        block = (rows, 128)
        return pl.pallas_call(
            functools.partial(kernel, n_ctx, n_tp),
            out_shape=(
                pltpu.VMEM(block, BF16),
                pltpu.VMEM(block, BF16),
            ),
            in_specs=[hbm] * 10,
            out_specs=(vmem, vmem),
            scratch_shapes=[
                pltpu.VMEM(block, BF16),
                pltpu.VMEM((3,) + block, BF16),
                pltpu.VMEM(sf.shape, F32),
                pltpu.VMEM(residues.shape[::-1], F32),
                pltpu.VMEM(rates.shape[::-1], F32),
                pltpu.VMEM((n_tp, 128), F32),
                pltpu.VMEM(table.shape, F32),
                pltpu.VMEM(base.shape, F32),
                pltpu.VMEM(ow.shape, BF16),
                pltpu.VMEM((width, 384), BF16),
                pltpu.VMEM((3, rows + 8, 128), F32),
                pltpu.VMEM(block, F32),
                pltpu.VMEM((8, 2 * rows, 128), F32),
                pltpu.VMEM((32, 128), F32),
                pltpu.VMEM((n_ctx, 32, 128), F32),
                pltpu.VMEM((n_tp // 2,) + block, F32),
                pltpu.VMEM((n_tp // 2,) + block, F32),
                pltpu.VMEM((n_tp // 2,) + block, BF16),
                pltpu.VMEM((n_tp // 2,) + block, BF16),
                pltpu.VMEM((n_tp,) + block, BF16),
                pltpu.VMEM((2, n_ctx) + block, BF16),
                dma((4,)),
                dma((8,)),
                dma((n_ctx,)),
                dma((n_ctx,)),
                dma((n_tp,)),
                dma((n_tp,)),
                dma((n_tp,)),
                dma((n_tp,)),
                dma((2, n_ctx)),
                dma((2, n_ctx)),
                dma((n_tp // 2,)),
                dma((n_tp // 2,)),
            ],
            compiler_params=pltpu.CompilerParams(
                collective_id=0, has_side_effects=True, vmem_limit_bytes=56 * 1024 * 1024
            ),
        )(
            resid,
            feats.transpose(1, 0, 2),
            sf,
            residues.T,
            rates.T,
            gain.reshape(n_tp, 128),
            jnp.asarray(table),
            jnp.asarray(base),
            ow,
            aw.transpose(1, 0, 2),
        )

    in_specs = (
        P("ctx", "tp"),
        P("ctx", None, "tp"),
        P(None, None, "tp"),
        P("tp", None),
        P("tp", None),
        P("tp", None),
        P(),
        P(None, None, "tp"),
    )
    return jax.shard_map(
        per_device,
        mesh=mesh,
        in_specs=in_specs,
        out_specs=(P("ctx", "tp"), P("ctx", "tp")),
        check_vma=False,
    )
```

```python
import functools
import math

import jax
import jax.numpy as jnp
import numpy as np
from jax import lax
from jax.experimental import pallas as pl
from jax.experimental.pallas import tpu as pltpu
from jax.sharding import PartitionSpec as P

HEAD_DIM = 128
EPS = 1e-05
ROPE_BASE = 10000.0
FILL = -1e30
MESH = pl.DeviceIdType.MESH
F32 = jnp.float32
BF16 = jnp.bfloat16


def kernel(
    n_ctx,
    n_tp,
    resid_hbm,
    feats_hbm,
    sf_hbm,
    res_hbm,
    rate_hbm,
    gain_hbm,
    table_hbm,
    base_hbm,
    ow_hbm,
    aw_hbm,
    hy_ref,
    ctx_ref,
    resid_ref,
    feats_ref,
    sf_ref,
    res_ref,
    rate_ref,
    gain_ref,
    table_ref,
    base_ref,
    ow,
    aw,
    xpad,
    prod,
    fsh,
    msg,
    msg_in,
    pair_out,
    pair_in,
    part_out,
    part_in,
    gath,
    kv,
    w_sem,
    in_sem,
    s1,
    r1,
    s2,
    r2,
    s3,
    r3,
    s4,
    r4,
    s5,
    r5,
):
    me_c = lax.axis_index("ctx")
    me_t = lax.axis_index("tp")
    rows = resid_ref.shape[0]
    modes = res_ref.shape[0]
    width = n_tp * 128
    tiles = rows // 8
    n_chip = n_tp // 2
    core = lax.rem(me_t, 2)
    chip = me_t // 2
    partner = chip * 2 + 1 - core

    def same_core(d):
        return lax.rem(chip + d, n_chip) * 2 + core

    in_copies = []
    for i, (src, dst) in enumerate(
        (
            (feats_hbm, feats_ref),
            (sf_hbm, sf_ref),
            (rate_hbm, rate_ref),
            (res_hbm, res_ref),
            (table_hbm, table_ref),
            (base_hbm, base_ref),
            (resid_hbm, resid_ref),
            (gain_hbm, gain_ref),
        )
    ):
        in_copies.append(pltpu.make_async_copy(src, dst, in_sem.at[i]))
    for c in in_copies:
        c.start()

    barrier = pltpu.get_barrier_semaphore()
    for peer in [partner] + [same_core(d) for d in range(1, n_chip)]:
        pl.semaphore_signal(barrier, inc=1, device_id={"tp": peer}, device_id_type=MESH)
    for d in range(1, n_ctx):

        @pl.when(me_c >= d)
        def _(d=d):
            pl.semaphore_signal(
                barrier, inc=1, device_id={"ctx": me_c - d}, device_id_type=MESH
            )

    w_copies = [pltpu.make_async_copy(ow_hbm, ow, w_sem.at[0])]
    for slot, p in enumerate((1, 2, 0)):
        w_copies.append(
            pltpu.make_async_copy(
                aw_hbm.at[p], aw.at[:, pl.ds(slot * 128, 128)], w_sem.at[1 + slot]
            )
        )
    for c in w_copies:
        c.start()

    for c in in_copies[0:3]:
        c.wait()

    short = []
    for p in range(3):
        x = feats_ref[p].astype(F32)
        xpad[p, 0:8, :] = jnp.zeros((8, 128), F32)
        xpad[p, pl.ds(8, rows), :] = x
        short.append(
            sf_ref[0, p : p + 1, :] * x
            + sf_ref[1, p : p + 1, :] * xpad[p, pl.ds(7, rows), :]
            + sf_ref[2, p : p + 1, :] * xpad[p, pl.ds(6, rows), :]
        )
    row_id = lax.broadcasted_iota(jnp.int32, (rows, 128), 0)
    p_mask = jnp.where(row_id >= 2, (short[1] * short[2]).astype(BF16).astype(F32), 0.0)
    prod[...] = p_mask

    rates = rate_ref[...]
    eight = lax.broadcasted_iota(jnp.int32, (8, 128), 0).astype(F32)
    lam8 = jnp.exp(-8.0 * rates)

    for m in range(modes):
        state = p_mask[0:8]
        for i in range(1, tiles):
            state = state * lam8[m : m + 1] + p_mask[8 * i : 8 * i + 8]
        state = state * jnp.exp(-rates[m : m + 1] * (7.0 - eight))
        msg[m : m + 1, :] = jnp.sum(state, axis=0, keepdims=True)
    for p in range(3):
        msg[16 + 2 * p : 18 + 2 * p, :] = xpad[p, rows + 6 : rows + 8, :]
    for p in range(1, 3):
        msg[20 + 2 * p : 22 + 2 * p, :] = xpad[p, 8:10, :]
    msg[26:32, :] = jnp.zeros((6, 128), F32)

    pl.semaphore_wait(barrier, n_chip + (n_ctx - 1 - me_c))

    def msg_copy(d):
        return pltpu.make_async_remote_copy(
            src_ref=msg,
            dst_ref=msg_in.at[me_c],
            send_sem=s1.at[d],
            recv_sem=r1.at[me_c],
            device_id={"ctx": me_c + d},
            device_id_type=MESH,
        )

    for d in range(1, n_ctx):

        @pl.when(me_c + d < n_ctx)
        def _(d=d):
            msg_copy(d).start()

    for c in in_copies[3:]:
        c.wait()
    weight = res_ref[...] * jnp.sqrt(1.0 - jnp.exp(-2.0 * rates))
    taps = [jnp.zeros((8, 128), F32) for _ in range(tiles)]
    for m in range(modes):
        e = weight[m : m + 1] * jnp.exp(-rates[m : m + 1] * eight)
        for i in range(tiles):
            taps[i] = taps[i] + e
            e = e * lam8[m : m + 1]
    taps = jnp.concatenate(taps, axis=0)
    for r in range(8):
        fsh[r, 0 : rows + 8, :] = jnp.zeros((rows + 8, 128), F32)
        fsh[r, rows + r : 2 * rows, :] = taps[0 : rows - r]

    def conv_step(j, acc):
        start = pl.multiple_of(rows - 8 * j, 8)
        block = prod[pl.ds(pl.multiple_of(8 * j, 8), 8), :]
        for r in range(8):
            acc = acc + fsh[r, pl.ds(start, rows), :] * block[r : r + 1]
        return acc

    def conv_step_low(j, acc):
        start = pl.multiple_of(rows + rows // 2 - 8 * j, 8)
        block = prod[pl.ds(pl.multiple_of(8 * j, 8), 8), :]
        for r in range(8):
            acc = acc + fsh[r, pl.ds(start, rows // 2), :] * block[r : r + 1]
        return acc

    conv = lax.fori_loop(0, tiles // 2, conv_step, jnp.zeros((rows, 128), F32))
    low = lax.fori_loop(tiles // 2, tiles, conv_step_low, conv[rows // 2 :])
    conv = jnp.concatenate([conv[: rows // 2], low], axis=0)

    for k in range(1, n_ctx):

        @pl.when(k > me_c)
        def _(k=k):
            kv[0, k] = jnp.zeros((rows, 128), BF16)
            kv[1, k] = jnp.zeros((rows, 128), BF16)

    cos_l, sin_l = table_ref[0], table_ref[1]
    cos_b = base_ref[0, pl.ds(me_c, 1), :]
    sin_b = base_ref[1, pl.ds(me_c, 1), :]
    lane = lax.broadcasted_iota(jnp.int32, (rows, 128), 1)
    cosine = cos_b * cos_l - sin_b * sin_l
    sine = sin_b * cos_l + cos_b * sin_l
    sine = jnp.where(lane < 64, -sine, sine)

    span = float(rows)
    lam_full = jnp.exp(-span * rates)
    lam_p0 = jnp.exp(-(span - 1.0) * rates)
    lam_p1 = jnp.exp(-(span - 2.0) * rates)

    def tap(j, p):
        return sf_ref[j, p : p + 1, :]

    def first_rows(p, x0, x1, h0, h1):
        a = tap(0, p) * x0 + tap(1, p) * h1 + tap(2, p) * h0
        b = tap(0, p) * x1 + tap(1, p) * x0 + tap(2, p) * h1
        return a, b

    def first_products(kx, vx, halo):
        k0, k1 = first_rows(1, kx[0], kx[1], halo[2], halo[3])
        v0, v1 = first_rows(2, vx[0], vx[1], halo[4], halo[5])
        return (k0 * v0).astype(BF16).astype(F32), (k1 * v1).astype(BF16).astype(F32)

    def state_step(k, carried):
        total, halo = carried
        pltpu.make_async_remote_copy(
            src_ref=msg,
            dst_ref=msg_in.at[k],
            send_sem=s1.at[0],
            recv_sem=r1.at[k],
            device_id={"ctx": k},
            device_id_type=MESH,
        ).wait_recv()
        got = [msg_in[k, i : i + 1, :] for i in range(16, 26)]
        p0, p1 = first_products(got[6:8], got[8:10], halo)
        total = total * lam_full + msg_in[k, 0:modes, :] + lam_p0 * p0 + lam_p1 * p1
        return total, tuple(got[0:6])

    zero_row = jnp.zeros((1, 128), F32)
    total, halo = lax.fori_loop(
        0, me_c, state_step, (jnp.zeros((modes, 128), F32), (zero_row,) * 6)
    )
    p0, p1 = first_products(
        [xpad[1, 8:9, :], xpad[1, 9:10, :]], [xpad[2, 8:9, :], xpad[2, 9:10, :]], halo
    )
    q0, q1 = first_rows(0, xpad[0, 8:9, :], xpad[0, 9:10, :], halo[0], halo[1])
    total = total * weight
    cross = [jnp.zeros((8, 128), F32) for _ in range(tiles)]
    for m in range(modes):
        e = total[m : m + 1] * jnp.exp(-rates[m : m + 1] * (eight + 1.0))
        for i in range(tiles):
            cross[i] = cross[i] + e
            e = e * lam8[m : m + 1]
    conv = conv + jnp.concatenate(cross, axis=0)
    conv = conv + fsh[0, pl.ds(rows, rows), :] * p0 + fsh[1, pl.ds(rows, rows), :] * p1
    query_part = jnp.where(row_id == 0, q0, jnp.where(row_id == 1, q1, short[0]))
    gated = (query_part * conv).astype(BF16)

    w_copies[0].wait()

    half = rows // 2

    def pair_copy(h, d):
        return pltpu.make_async_remote_copy(
            src_ref=pair_out.at[d, pl.ds(h * half, half)],
            dst_ref=pair_in.at[d, pl.ds(h * half, half)],
            send_sem=s5.at[h, d],
            recv_sem=r5.at[h, d],
            device_id={"tp": partner},
            device_id_type=MESH,
        )

    def part_copy(h, d):
        return pltpu.make_async_remote_copy(
            src_ref=part_out.at[d, pl.ds(h * half, half)],
            dst_ref=part_in.at[d, pl.ds(h * half, half)],
            send_sem=s2.at[h, d],
            recv_sem=r2.at[h, d],
            device_id={"tp": same_core(d)},
            device_id_type=MESH,
        )

    def gath_copy(h, sem, owner, target):
        return pltpu.make_async_remote_copy(
            src_ref=gath.at[owner, pl.ds(h * half, half)],
            dst_ref=gath.at[owner, pl.ds(h * half, half)],
            send_sem=s3.at[h, sem],
            recv_sem=r3.at[h, owner],
            device_id={"tp": target},
            device_id_type=MESH,
        )

    mine = [[None] * n_chip for _ in range(2)]
    for h in range(2):
        now = slice(h * half, (h + 1) * half)
        for d in list(range(1, n_chip)) + [0]:
            start = pl.multiple_of(lax.rem(chip + d, n_chip) * 256, 256)
            both = jnp.dot(gated[now], ow[:, pl.ds(start, 256)], preferred_element_type=F32)
            pair_out[d, now] = jnp.where(core == 0, both[:, 128:256], both[:, 0:128])
            pair_copy(h, d).start()
            mine[h][d] = jnp.where(core == 0, both[:, 0:128], both[:, 128:256])
    for h in range(2):
        now = slice(h * half, (h + 1) * half)
        for d in range(1, n_chip):
            pair_copy(h, d).wait_recv()
            part_out[d, now] = (mine[h][d] + pair_in[d, now]).astype(BF16)
            part_copy(h, d).start()
    for h in range(2):
        now = slice(h * half, (h + 1) * half)
        pair_copy(h, 0).wait_recv()
        mix = resid_ref[now].astype(F32) + (mine[h][0] + pair_in[0, now])
        for d in range(1, n_chip):
            part_copy(h, d).wait_recv()
            mix = mix + part_in[d, now].astype(F32)
        hyena = mix.astype(BF16)
        gath[me_t, now] = hyena
        for d in range(1, n_chip):
            gath_copy(h, d, me_t, same_core(d)).start()
        gath_copy(h, 0, me_t, partner).start()
        hy_ref[now] = hyena
    for c in w_copies[1:]:
        c.wait()

    def chip_block(t, square, key_value, query):
        scaled = []
        for i in range(2):
            wide = gath[2 * t + i].astype(F32)
            square = square + wide * wide
            scaled.append((wide * gain_ref[pl.ds(2 * t + i, 1), :]).astype(BF16))
        scaled = jnp.concatenate(scaled, axis=1)
        weights = pl.ds(pl.multiple_of(t * 256, 256), 256)
        key_value = key_value + jnp.dot(scaled, aw[weights, 0:256], preferred_element_type=F32)
        query = query + jnp.dot(scaled, aw[weights, 256:384], preferred_element_type=F32)
        return square, key_value, query

    for h in range(2):
        gath_copy(h, 0, partner, partner).wait_recv()
    sums = chip_block(
        chip,
        jnp.zeros((rows, 128), F32),
        jnp.zeros((rows, 256), F32),
        jnp.zeros((rows, 128), F32),
    )
    for h in range(2):
        for d in range(1, n_chip):
            owner = same_core(n_chip - d)
            gath_copy(h, d, owner, partner).wait_recv()
            gath_copy(h, n_chip + d, owner, partner).start()
    for d in range(1, n_chip):
        source = lax.rem(chip + n_chip - d, n_chip)
        for h in range(2):
            gath_copy(h, d, source * 2 + 1 - core, partner).wait_recv()
        sums = chip_block(source, *sums)
    square, key_value, query = sums
    scale = lax.rsqrt(jnp.sum(square, axis=1, keepdims=True) / float(width) + EPS)

    def turned(x):
        return (x * cosine + pltpu.roll(x, 64, axis=1) * sine).astype(BF16)

    kv[0, me_c] = turned(key_value[:, 0:128] * scale)
    kv[1, me_c] = (key_value[:, 128:256] * scale).astype(BF16)

    def kv_copy(which, d, owner, target):
        return pltpu.make_async_remote_copy(
            src_ref=kv.at[which, owner],
            dst_ref=kv.at[which, owner],
            send_sem=s4.at[which, d],
            recv_sem=r4.at[which, owner],
            device_id={"ctx": target},
            device_id_type=MESH,
        )

    for which in range(2):
        for d in range(1, n_ctx):

            @pl.when(me_c + d < n_ctx)
            def _(which=which, d=d):
                kv_copy(which, d, me_c, me_c + d).start()

    queries = turned(query * scale)
    factor = 1.0 / math.sqrt(HEAD_DIM)
    keys_n = n_ctx * rows

    def arrived(which):
        for k in range(n_ctx - 1):

            @pl.when(k < me_c)
            def _(k=k):
                kv_copy(which, 0, k, k).wait_recv()

    row_pos = me_c * rows + lax.broadcasted_iota(jnp.int32, (rows, keys_n), 0)
    allowed = row_pos >= lax.broadcasted_iota(jnp.int32, (rows, keys_n), 1)
    arrived(0)
    scores = (
        lax.dot_general(
            queries,
            kv[0].reshape(keys_n, 128),
            (((1,), (1,)), ((), ())),
            preferred_element_type=F32,
        )
        * factor
    )
    scores = jnp.where(allowed, scores, FILL)
    probs = jnp.exp(scores - jnp.max(scores, axis=1, keepdims=True))
    probs = jnp.where(allowed, probs, 0.0)
    total_p = jnp.sum(probs, axis=1, keepdims=True)
    arrived(1)
    acc = jnp.dot(
        probs.astype(BF16), kv[1].reshape(keys_n, 128), preferred_element_type=F32
    )
    ctx_ref[...] = (acc / total_p).astype(BF16)

    for h in range(2):
        for d in range(n_chip):
            pair_copy(h, d).wait_send()
            gath_copy(h, d, me_t, partner).wait_send()
            if d > 0:
                part_copy(h, d).wait_send()
                gath_copy(h, n_chip + d, me_t, partner).wait_send()
    for d in range(1, n_ctx):

        @pl.when(me_c + d < n_ctx)
        def _(d=d):
            msg_copy(d).wait_send()
            kv_copy(0, d, me_c, me_c + d).wait_send()
            kv_copy(1, d, me_c, me_c + d).wait_send()


def rotary_tables(rows, n_ctx):
    half = HEAD_DIM // 2
    freq = ROPE_BASE ** (-np.arange(half, dtype=np.float64) * 2.0 / HEAD_DIM)
    freq = np.concatenate([freq, freq])
    local = np.arange(rows)[:, None] * freq
    base = (np.arange(n_ctx) * rows)[:, None] * freq
    table = np.stack([np.cos(local), np.sin(local)]).astype(np.float32)
    return table, np.stack([np.cos(base), np.sin(base)]).astype(np.float32)


def solution(mesh):
    n_ctx, n_tp = mesh.shape["ctx"], mesh.shape["tp"]

    def per_device(resid, feats, sf, residues, rates, ow, gain, aw):
        rows = resid.shape[0]
        width = ow.shape[1]
        table, base = rotary_tables(rows, n_ctx)
        vmem = pl.BlockSpec(memory_space=pltpu.VMEM)
        hbm = pl.BlockSpec(memory_space=pltpu.HBM)
        dma = pltpu.SemaphoreType.DMA
        block = (rows, 128)
        return pl.pallas_call(
            functools.partial(kernel, n_ctx, n_tp),
            out_shape=(
                pltpu.VMEM(block, BF16),
                pltpu.VMEM(block, BF16),
            ),
            in_specs=[hbm] * 10,
            out_specs=(vmem, vmem),
            scratch_shapes=[
                pltpu.VMEM(block, BF16),
                pltpu.VMEM((3,) + block, BF16),
                pltpu.VMEM(sf.shape, F32),
                pltpu.VMEM(residues.shape[::-1], F32),
                pltpu.VMEM(rates.shape[::-1], F32),
                pltpu.VMEM((n_tp, 128), F32),
                pltpu.VMEM(table.shape, F32),
                pltpu.VMEM(base.shape, F32),
                pltpu.VMEM(ow.shape, BF16),
                pltpu.VMEM((width, 384), BF16),
                pltpu.VMEM((3, rows + 8, 128), F32),
                pltpu.VMEM(block, F32),
                pltpu.VMEM((8, 2 * rows, 128), F32),
                pltpu.VMEM((32, 128), F32),
                pltpu.VMEM((n_ctx, 32, 128), F32),
                pltpu.VMEM((n_tp // 2,) + block, F32),
                pltpu.VMEM((n_tp // 2,) + block, F32),
                pltpu.VMEM((n_tp // 2,) + block, BF16),
                pltpu.VMEM((n_tp // 2,) + block, BF16),
                pltpu.VMEM((n_tp,) + block, BF16),
                pltpu.VMEM((2, n_ctx) + block, BF16),
                dma((4,)),
                dma((8,)),
                dma((n_ctx,)),
                dma((n_ctx,)),
                dma((2, n_tp)),
                dma((2, n_tp)),
                dma((2, n_tp)),
                dma((2, n_tp)),
                dma((2, n_ctx)),
                dma((2, n_ctx)),
                dma((2, n_tp // 2)),
                dma((2, n_tp // 2)),
            ],
            compiler_params=pltpu.CompilerParams(
                collective_id=0, has_side_effects=True, vmem_limit_bytes=56 * 1024 * 1024
            ),
        )(
            resid,
            feats.transpose(1, 0, 2),
            sf,
            residues.T,
            rates.T,
            gain.reshape(n_tp, 128),
            jnp.asarray(table),
            jnp.asarray(base),
            ow,
            aw.transpose(1, 0, 2),
        )

    in_specs = (
        P("ctx", "tp"),
        P("ctx", None, "tp"),
        P(None, None, "tp"),
        P("tp", None),
        P("tp", None),
        P("tp", None),
        P(),
        P(None, None, "tp"),
    )
    return jax.shard_map(
        per_device,
        mesh=mesh,
        in_specs=in_specs,
        out_specs=(P("ctx", "tp"), P("ctx", "tp")),
        check_vma=False,
    )
```

```python
import functools
import math

import jax
import jax.numpy as jnp
import numpy as np
from jax import lax
from jax.experimental import pallas as pl
from jax.experimental.pallas import tpu as pltpu
from jax.sharding import PartitionSpec as P

HEAD_DIM = 128
EPS = 1e-05
ROPE_BASE = 10000.0
FILL = -1e30
MESH = pl.DeviceIdType.MESH
F32 = jnp.float32
BF16 = jnp.bfloat16


def kernel(
    n_ctx,
    n_tp,
    resid_hbm,
    feats_hbm,
    sf_hbm,
    res_hbm,
    rate_hbm,
    gain_hbm,
    table_hbm,
    base_hbm,
    ow_hbm,
    aw_hbm,
    hy_ref,
    ctx_ref,
    resid_ref,
    feats_ref,
    sf_ref,
    res_ref,
    rate_ref,
    gain_ref,
    table_ref,
    base_ref,
    ow,
    aw,
    xpad,
    prod,
    fsh,
    msg,
    msg_in,
    pair_out,
    pair_in,
    part_out,
    part_in,
    gath,
    kv,
    w_sem,
    in_sem,
    s1,
    r1,
    s2,
    r2,
    s3,
    r3,
    s4,
    r4,
    s5,
    r5,
):
    me_c = lax.axis_index("ctx")
    me_t = lax.axis_index("tp")
    rows = resid_ref.shape[0]
    modes = res_ref.shape[0]
    width = n_tp * 128
    tiles = rows // 8
    n_chip = n_tp // 2
    core = lax.rem(me_t, 2)
    chip = me_t // 2
    partner = chip * 2 + 1 - core

    def same_core(d):
        return lax.rem(chip + d, n_chip) * 2 + core

    in_copies = []
    for i, (src, dst) in enumerate(
        (
            (feats_hbm, feats_ref),
            (sf_hbm, sf_ref),
            (rate_hbm, rate_ref),
            (res_hbm, res_ref),
            (table_hbm, table_ref),
            (base_hbm, base_ref),
            (resid_hbm, resid_ref),
            (gain_hbm, gain_ref),
        )
    ):
        in_copies.append(pltpu.make_async_copy(src, dst, in_sem.at[i]))
    for c in in_copies:
        c.start()

    barrier = pltpu.get_barrier_semaphore()
    for peer in [partner] + [same_core(d) for d in range(1, n_chip)]:
        pl.semaphore_signal(barrier, inc=1, device_id={"tp": peer}, device_id_type=MESH)
    for d in range(1, n_ctx):

        @pl.when(me_c >= d)
        def _(d=d):
            pl.semaphore_signal(
                barrier, inc=1, device_id={"ctx": me_c - d}, device_id_type=MESH
            )

    w_copies = [pltpu.make_async_copy(ow_hbm, ow, w_sem.at[0])]
    for slot, p in enumerate((1, 2, 0)):
        w_copies.append(
            pltpu.make_async_copy(
                aw_hbm.at[p], aw.at[:, pl.ds(slot * 128, 128)], w_sem.at[1 + slot]
            )
        )
    for c in w_copies:
        c.start()

    for c in in_copies[0:3]:
        c.wait()

    short = []
    for p in range(3):
        x = feats_ref[p].astype(F32)
        xpad[p, 0:8, :] = jnp.zeros((8, 128), F32)
        xpad[p, pl.ds(8, rows), :] = x
        short.append(
            sf_ref[0, p : p + 1, :] * x
            + sf_ref[1, p : p + 1, :] * xpad[p, pl.ds(7, rows), :]
            + sf_ref[2, p : p + 1, :] * xpad[p, pl.ds(6, rows), :]
        )
    row_id = lax.broadcasted_iota(jnp.int32, (rows, 128), 0)
    p_mask = jnp.where(row_id >= 2, (short[1] * short[2]).astype(BF16).astype(F32), 0.0)
    prod[...] = p_mask

    rates = rate_ref[...]
    eight = lax.broadcasted_iota(jnp.int32, (8, 128), 0).astype(F32)
    lam8 = jnp.exp(-8.0 * rates)

    for m in range(modes):
        state = p_mask[0:8]
        for i in range(1, tiles):
            state = state * lam8[m : m + 1] + p_mask[8 * i : 8 * i + 8]
        state = state * jnp.exp(-rates[m : m + 1] * (7.0 - eight))
        msg[m : m + 1, :] = jnp.sum(state, axis=0, keepdims=True)
    for p in range(3):
        msg[16 + 2 * p : 18 + 2 * p, :] = xpad[p, rows + 6 : rows + 8, :]
    for p in range(1, 3):
        msg[20 + 2 * p : 22 + 2 * p, :] = xpad[p, 8:10, :]
    msg[26:32, :] = jnp.zeros((6, 128), F32)

    pl.semaphore_wait(barrier, n_chip + (n_ctx - 1 - me_c))

    def msg_copy(d):
        return pltpu.make_async_remote_copy(
            src_ref=msg,
            dst_ref=msg_in.at[me_c],
            send_sem=s1.at[d],
            recv_sem=r1.at[me_c],
            device_id={"ctx": me_c + d},
            device_id_type=MESH,
        )

    for d in range(1, n_ctx):

        @pl.when(me_c + d < n_ctx)
        def _(d=d):
            msg_copy(d).start()

    for c in in_copies[3:]:
        c.wait()
    weight = res_ref[...] * jnp.sqrt(1.0 - jnp.exp(-2.0 * rates))
    taps = [jnp.zeros((8, 128), F32) for _ in range(tiles)]
    for m in range(modes):
        e = weight[m : m + 1] * jnp.exp(-rates[m : m + 1] * eight)
        for i in range(tiles):
            taps[i] = taps[i] + e
            e = e * lam8[m : m + 1]
    taps = jnp.concatenate(taps, axis=0)
    for r in range(8):
        fsh[r, 0 : rows + 8, :] = jnp.zeros((rows + 8, 128), F32)
        fsh[r, rows + r : 2 * rows, :] = taps[0 : rows - r]

    def conv_step(j, acc):
        start = pl.multiple_of(rows - 8 * j, 8)
        block = prod[pl.ds(pl.multiple_of(8 * j, 8), 8), :]
        for r in range(8):
            acc = acc + fsh[r, pl.ds(start, rows), :] * block[r : r + 1]
        return acc

    def conv_step_low(j, acc):
        start = pl.multiple_of(rows + rows // 2 - 8 * j, 8)
        block = prod[pl.ds(pl.multiple_of(8 * j, 8), 8), :]
        for r in range(8):
            acc = acc + fsh[r, pl.ds(start, rows // 2), :] * block[r : r + 1]
        return acc

    conv = lax.fori_loop(0, tiles // 2, conv_step, jnp.zeros((rows, 128), F32))
    low = lax.fori_loop(tiles // 2, tiles, conv_step_low, conv[rows // 2 :])
    conv = jnp.concatenate([conv[: rows // 2], low], axis=0)

    for k in range(1, n_ctx):

        @pl.when(k > me_c)
        def _(k=k):
            kv[0, k] = jnp.zeros((rows, 128), BF16)
            kv[1, k] = jnp.zeros((rows, 128), BF16)

    cos_l, sin_l = table_ref[0], table_ref[1]
    cos_b = base_ref[0, pl.ds(me_c, 1), :]
    sin_b = base_ref[1, pl.ds(me_c, 1), :]
    lane = lax.broadcasted_iota(jnp.int32, (rows, 128), 1)
    cosine = cos_b * cos_l - sin_b * sin_l
    sine = sin_b * cos_l + cos_b * sin_l
    sine = jnp.where(lane < 64, -sine, sine)

    span = float(rows)
    lam_full = jnp.exp(-span * rates)
    lam_p0 = jnp.exp(-(span - 1.0) * rates)
    lam_p1 = jnp.exp(-(span - 2.0) * rates)

    def tap(j, p):
        return sf_ref[j, p : p + 1, :]

    def first_rows(p, x0, x1, h0, h1):
        a = tap(0, p) * x0 + tap(1, p) * h1 + tap(2, p) * h0
        b = tap(0, p) * x1 + tap(1, p) * x0 + tap(2, p) * h1
        return a, b

    def first_products(kx, vx, halo):
        k0, k1 = first_rows(1, kx[0], kx[1], halo[2], halo[3])
        v0, v1 = first_rows(2, vx[0], vx[1], halo[4], halo[5])
        return (k0 * v0).astype(BF16).astype(F32), (k1 * v1).astype(BF16).astype(F32)

    def state_step(k, carried):
        total, halo = carried
        pltpu.make_async_remote_copy(
            src_ref=msg,
            dst_ref=msg_in.at[k],
            send_sem=s1.at[0],
            recv_sem=r1.at[k],
            device_id={"ctx": k},
            device_id_type=MESH,
        ).wait_recv()
        got = [msg_in[k, i : i + 1, :] for i in range(16, 26)]
        p0, p1 = first_products(got[6:8], got[8:10], halo)
        total = total * lam_full + msg_in[k, 0:modes, :] + lam_p0 * p0 + lam_p1 * p1
        return total, tuple(got[0:6])

    zero_row = jnp.zeros((1, 128), F32)
    total, halo = lax.fori_loop(
        0, me_c, state_step, (jnp.zeros((modes, 128), F32), (zero_row,) * 6)
    )
    p0, p1 = first_products(
        [xpad[1, 8:9, :], xpad[1, 9:10, :]], [xpad[2, 8:9, :], xpad[2, 9:10, :]], halo
    )
    q0, q1 = first_rows(0, xpad[0, 8:9, :], xpad[0, 9:10, :], halo[0], halo[1])
    total = total * weight
    cross = [jnp.zeros((8, 128), F32) for _ in range(tiles)]
    for m in range(modes):
        e = total[m : m + 1] * jnp.exp(-rates[m : m + 1] * (eight + 1.0))
        for i in range(tiles):
            cross[i] = cross[i] + e
            e = e * lam8[m : m + 1]
    conv = conv + jnp.concatenate(cross, axis=0)
    conv = conv + fsh[0, pl.ds(rows, rows), :] * p0 + fsh[1, pl.ds(rows, rows), :] * p1
    query_part = jnp.where(row_id == 0, q0, jnp.where(row_id == 1, q1, short[0]))
    gated = (query_part * conv).astype(BF16)

    w_copies[0].wait()

    half = rows // 2

    def pair_copy(h, d):
        return pltpu.make_async_remote_copy(
            src_ref=pair_out.at[d, pl.ds(h * half, half)],
            dst_ref=pair_in.at[d, pl.ds(h * half, half)],
            send_sem=s5.at[h, d],
            recv_sem=r5.at[h, d],
            device_id={"tp": partner},
            device_id_type=MESH,
        )

    def part_copy(h, d):
        return pltpu.make_async_remote_copy(
            src_ref=part_out.at[d, pl.ds(h * half, half)],
            dst_ref=part_in.at[d, pl.ds(h * half, half)],
            send_sem=s2.at[h, d],
            recv_sem=r2.at[h, d],
            device_id={"tp": same_core(d)},
            device_id_type=MESH,
        )

    def gath_copy(h, sem, owner, target):
        return pltpu.make_async_remote_copy(
            src_ref=gath.at[owner, pl.ds(h * half, half)],
            dst_ref=gath.at[owner, pl.ds(h * half, half)],
            send_sem=s3.at[h, sem],
            recv_sem=r3.at[h, owner],
            device_id={"tp": target},
            device_id_type=MESH,
        )

    mine = [[None] * n_chip for _ in range(2)]
    for h in range(2):
        now = slice(h * half, (h + 1) * half)
        for d in list(range(1, n_chip)) + [0]:
            start = pl.multiple_of(lax.rem(chip + d, n_chip) * 256, 256)
            both = jnp.dot(gated[now], ow[:, pl.ds(start, 256)], preferred_element_type=F32)
            pair_out[d, now] = jnp.where(core == 0, both[:, 128:256], both[:, 0:128])
            pair_copy(h, d).start()
            mine[h][d] = jnp.where(core == 0, both[:, 0:128], both[:, 128:256])
    for h in range(2):
        now = slice(h * half, (h + 1) * half)
        for d in range(1, n_chip):
            pair_copy(h, d).wait_recv()
            part_out[d, now] = (mine[h][d] + pair_in[d, now]).astype(BF16)
            part_copy(h, d).start()
    for h in range(2):
        now = slice(h * half, (h + 1) * half)
        pair_copy(h, 0).wait_recv()
        mix = resid_ref[now].astype(F32) + (mine[h][0] + pair_in[0, now])
        for d in range(1, n_chip):
            part_copy(h, d).wait_recv()
            mix = mix + part_in[d, now].astype(F32)
        hyena = mix.astype(BF16)
        gath[me_t, now] = hyena
        for d in range(1, n_chip):
            gath_copy(h, d, me_t, same_core(d)).start()
        gath_copy(h, 0, me_t, partner).start()
        hy_ref[now] = hyena
    for c in w_copies[1:]:
        c.wait()

    def chip_block(t, square, key_value, query):
        scaled = []
        for i in range(2):
            wide = gath[2 * t + i].astype(F32)
            square = square + wide * wide
            scaled.append((wide * gain_ref[pl.ds(2 * t + i, 1), :]).astype(BF16))
        scaled = jnp.concatenate(scaled, axis=1)
        weights = pl.ds(pl.multiple_of(t * 256, 256), 256)
        key_value = key_value + jnp.dot(scaled, aw[weights, 0:256], preferred_element_type=F32)
        query = query + jnp.dot(scaled, aw[weights, 256:384], preferred_element_type=F32)
        return square, key_value, query

    for h in range(2):
        gath_copy(h, 0, partner, partner).wait_recv()
    sums = chip_block(
        chip,
        jnp.zeros((rows, 128), F32),
        jnp.zeros((rows, 256), F32),
        jnp.zeros((rows, 128), F32),
    )
    for h in range(2):
        for d in range(1, n_chip):
            owner = same_core(n_chip - d)
            gath_copy(h, d, owner, partner).wait_recv()
            gath_copy(h, n_chip + d, owner, partner).start()
    for d in range(1, n_chip):
        source = lax.rem(chip + n_chip - d, n_chip)
        for h in range(2):
            gath_copy(h, d, source * 2 + 1 - core, partner).wait_recv()
        sums = chip_block(source, *sums)
    square, key_value, query = sums
    scale = lax.rsqrt(jnp.sum(square, axis=1, keepdims=True) / float(width) + EPS)

    def turned(x):
        return (x * cosine + pltpu.roll(x, 64, axis=1) * sine).astype(BF16)

    kv[0, me_c] = turned(key_value[:, 0:128] * scale)
    kv[1, me_c] = (key_value[:, 128:256] * scale).astype(BF16)

    def kv_copy(which, d, owner, target):
        return pltpu.make_async_remote_copy(
            src_ref=kv.at[which, owner],
            dst_ref=kv.at[which, owner],
            send_sem=s4.at[which, d],
            recv_sem=r4.at[which, owner],
            device_id={"ctx": target},
            device_id_type=MESH,
        )

    for which in range(2):
        for d in range(1, n_ctx):

            @pl.when(me_c + d < n_ctx)
            def _(which=which, d=d):
                kv_copy(which, d, me_c, me_c + d).start()

    queries = turned(query * scale)
    factor = 1.0 / math.sqrt(HEAD_DIM)
    keys_n = n_ctx * rows

    def arrived(which):
        for k in range(n_ctx - 1):

            @pl.when(k < me_c)
            def _(k=k):
                kv_copy(which, 0, k, k).wait_recv()

    row_pos = me_c * rows + lax.broadcasted_iota(jnp.int32, (rows, keys_n), 0)
    allowed = row_pos >= lax.broadcasted_iota(jnp.int32, (rows, keys_n), 1)
    arrived(0)
    scores = (
        lax.dot_general(
            queries,
            kv[0].reshape(keys_n, 128),
            (((1,), (1,)), ((), ())),
            preferred_element_type=F32,
        )
        * factor
    )
    scores = jnp.where(allowed, scores, FILL)
    probs = jnp.exp(scores - jnp.max(scores, axis=1, keepdims=True))
    probs = jnp.where(allowed, probs, 0.0)
    total_p = jnp.sum(probs, axis=1, keepdims=True)
    arrived(1)
    acc = jnp.dot(
        probs.astype(BF16), kv[1].reshape(keys_n, 128), preferred_element_type=F32
    )
    ctx_ref[...] = (acc / total_p).astype(BF16)

    for h in range(2):
        for d in range(n_chip):
            pair_copy(h, d).wait_send()
            gath_copy(h, d, me_t, partner).wait_send()
            if d > 0:
                part_copy(h, d).wait_send()
                gath_copy(h, n_chip + d, me_t, partner).wait_send()
    for d in range(1, n_ctx):

        @pl.when(me_c + d < n_ctx)
        def _(d=d):
            msg_copy(d).wait_send()
            kv_copy(0, d, me_c, me_c + d).wait_send()
            kv_copy(1, d, me_c, me_c + d).wait_send()


def store_kernel(a_ref, b_ref, a_hbm, b_hbm, sem):
    first = pltpu.make_async_copy(a_ref, a_hbm, sem.at[0])
    second = pltpu.make_async_copy(b_ref, b_hbm, sem.at[1])
    first.start()
    second.start()
    first.wait()
    second.wait()


def rotary_tables(rows, n_ctx):
    half = HEAD_DIM // 2
    freq = ROPE_BASE ** (-np.arange(half, dtype=np.float64) * 2.0 / HEAD_DIM)
    freq = np.concatenate([freq, freq])
    local = np.arange(rows)[:, None] * freq
    base = (np.arange(n_ctx) * rows)[:, None] * freq
    table = np.stack([np.cos(local), np.sin(local)]).astype(np.float32)
    return table, np.stack([np.cos(base), np.sin(base)]).astype(np.float32)


def solution(mesh):
    n_ctx, n_tp = mesh.shape["ctx"], mesh.shape["tp"]

    def per_device(resid, feats, sf, residues, rates, ow, gain, aw):
        rows = resid.shape[0]
        width = ow.shape[1]
        table, base = rotary_tables(rows, n_ctx)
        vmem = pl.BlockSpec(memory_space=pltpu.VMEM)
        hbm = pl.BlockSpec(memory_space=pltpu.HBM)
        dma = pltpu.SemaphoreType.DMA
        block = (rows, 128)
        results = pl.pallas_call(
            functools.partial(kernel, n_ctx, n_tp),
            out_shape=(
                pltpu.VMEM(block, BF16),
                pltpu.VMEM(block, BF16),
            ),
            in_specs=[hbm] * 10,
            out_specs=(vmem, vmem),
            scratch_shapes=[
                pltpu.VMEM(block, BF16),
                pltpu.VMEM((3,) + block, BF16),
                pltpu.VMEM(sf.shape, F32),
                pltpu.VMEM(residues.shape[::-1], F32),
                pltpu.VMEM(rates.shape[::-1], F32),
                pltpu.VMEM((n_tp, 128), F32),
                pltpu.VMEM(table.shape, F32),
                pltpu.VMEM(base.shape, F32),
                pltpu.VMEM(ow.shape, BF16),
                pltpu.VMEM((width, 384), BF16),
                pltpu.VMEM((3, rows + 8, 128), F32),
                pltpu.VMEM(block, F32),
                pltpu.VMEM((8, 2 * rows, 128), F32),
                pltpu.VMEM((32, 128), F32),
                pltpu.VMEM((n_ctx, 32, 128), F32),
                pltpu.VMEM((n_tp // 2,) + block, F32),
                pltpu.VMEM((n_tp // 2,) + block, F32),
                pltpu.VMEM((n_tp // 2,) + block, BF16),
                pltpu.VMEM((n_tp // 2,) + block, BF16),
                pltpu.VMEM((n_tp,) + block, BF16),
                pltpu.VMEM((2, n_ctx) + block, BF16),
                dma((4,)),
                dma((8,)),
                dma((n_ctx,)),
                dma((n_ctx,)),
                dma((2, n_tp)),
                dma((2, n_tp)),
                dma((2, n_tp)),
                dma((2, n_tp)),
                dma((2, n_ctx)),
                dma((2, n_ctx)),
                dma((2, n_tp // 2)),
                dma((2, n_tp // 2)),
            ],
            compiler_params=pltpu.CompilerParams(
                collective_id=0, has_side_effects=True, vmem_limit_bytes=56 * 1024 * 1024
            ),
        )(
            resid,
            feats.transpose(1, 0, 2),
            sf,
            residues.T,
            rates.T,
            gain.reshape(n_tp, 128),
            jnp.asarray(table),
            jnp.asarray(base),
            ow,
            aw.transpose(1, 0, 2),
        )
        return pl.pallas_call(
            store_kernel,
            out_shape=tuple(jax.ShapeDtypeStruct(block, BF16) for _ in range(2)),
            in_specs=[vmem, vmem],
            out_specs=(hbm, hbm),
            scratch_shapes=[dma((2,))],
        )(*[pltpu.with_memory_space_constraint(x, pltpu.VMEM) for x in results])

    in_specs = (
        P("ctx", "tp"),
        P("ctx", None, "tp"),
        P(None, None, "tp"),
        P("tp", None),
        P("tp", None),
        P("tp", None),
        P(),
        P(None, None, "tp"),
    )
    return jax.shard_map(
        per_device,
        mesh=mesh,
        in_specs=in_specs,
        out_specs=(P("ctx", "tp"), P("ctx", "tp")),
        check_vma=False,
    )
```
